768 devices in a mesh: lat: 96 (over z_lo, y, x), lon: 8 (over z_hi, core).
Axes of the slice: x: 4, y: 8, z: 12 (z_hi: 4, z_lo: 3; z = z_hi * 3 + z_lo), core: 2. Of those that a mesh axis runs over, the one named last changes fastest.
Arguments:
- grad_output: bfloat16 [768, 1440, 128], P('lat', 'lon'), may hold values from -6 to 6
- band_rows: int32 [96], replicated, may hold values from 1 to 8, 721 in all
- legendre: float32 [192, 360, 768], P('lat'), may hold values from -0.21875 to 0.21875
- quad_weights: float32 [768], replicated, may hold values from 0.3 to 3
- spectral_filter: float32 [2, 360, 128], replicated, may hold values from -6 to 6
- disco_kernel: float32 [768, 9, 9], replicated, may hold values from -2 to 2
- disco_weight: bfloat16 [128, 9, 128], replicated, may hold values from -0.1875 to 0.1875
Outputs:
- grad_input: bfloat16 [768, 1440, 128], P('lat', 'lon')
The draws below stay inside these ranges and needn't reach their ends.
Inputs may be any that keep to these rules, and one draw needn't show every extreme that they name: Bands follow each other from north to south; the live rows of band b fill its first band_rows[b] slots, and all bands together hold 721 rows.
All inputs are finite; a program needn't handle non-finite values.
Results may differ from the reference program's by a relative error of at most 0.0048.
Values may be sent and summed in bfloat16 or wider, within the bound.
A program may use at most 64 MiB of HBM per device.

```python
import math
import jax
import jax.numpy as jnp
import numpy as np
from jax import lax

C = 128
K = 9
TAPS = 9
M = 192
L = 360
ROWS_DEV = 8
BANDS = 96
NLAT = 768
LIVE = 721
NLON = 1440
N_LAT = 96


def level_of(rng, shape, pieces, least, high):
    def one(dim, shards_of):
        draws = jax.random.uniform(jax.random.fold_in(jax.random.fold_in(rng, 6), dim), (shards_of,), jnp.float32, least / len(pieces), high / len(pieces))
        return jnp.repeat(jnp.exp(draws), shape[dim] // shards_of).reshape((-1,) + (1,) * (len(shape) - dim - 1))

    loudness = one(*pieces[0])
    for cut in pieces[1:]:
        loudness = loudness * one(*cut)
    return loudness


def split_up(number_of, total, limit, lean):
    weights = [(1 << 20) // math.isqrt(grade ** lean) + 1 for grade in range(2, number_of + 1)]
    rest, counts = total - limit - (number_of - 1), [1] * (number_of - 1)
    while rest > 0:
        candidates = [i for i in range(number_of - 1) if counts[i] < limit]
        mass, left = sum([weights[i] for i in candidates]), rest
        for i in candidates:
            extra = min(limit - counts[i], max(1, left * weights[i] // mass), rest)
            counts[i] = counts[i] + extra
            rest = rest - extra
    return np.array([limit] + counts)


def ragged(rng, count, total, limit, lean):
    if count == 2:
        one = jax.random.randint(rng, (), max(1, total - limit), min(limit, total - 1) + 1)
        return jnp.stack([one, total - one])
    tallies = jnp.asarray(split_up(count, total, limit, lean), jnp.int32)
    twos = (count - 1) // 2
    donor, taker = tallies[1:1 + 2 * twos:2], tallies[2:2 + 2 * twos:2]
    room = jnp.minimum(donor - 1, limit - taker)
    moved = jax.random.randint(jax.random.fold_in(rng, 1), (twos,), 0, 1 << 20) % (room + 1)
    tallies = tallies.at[1:1 + 2 * twos:2].set(donor - moved).at[2:2 + 2 * twos:2].set(taker + moved)
    return tallies[jax.random.permutation(jax.random.fold_in(rng, 2), count)]


def bell_draw(own_key, shape, width, reach, cuts=(), kind=jnp.bfloat16):
    level = level_of(own_key, shape, cuts, -0.22, 0.18) if cuts else 1.0
    values = jax.random.normal(own_key, shape, jnp.float32) * width * level
    return jnp.minimum(jnp.maximum(values, -reach), reach).astype(kind)


def setup_inputs(seed: int = 0) -> dict:
    arg_keys = jax.random.split(jax.random.key(seed), 8)
    return {
        "grad_output": bell_draw(arg_keys[0], (NLAT, NLON, C), 1.0, 6.0, ((0, 96), (1, 8))),
        "band_rows": ragged(arg_keys[1], BANDS, LIVE, ROWS_DEV, 2).astype(jnp.int32),
        "legendre": bell_draw(arg_keys[2], (M, L, NLAT), LIVE ** -0.5, 0.21875, ((0, 96),), jnp.float32),
        "quad_weights": jnp.clip(jnp.exp(jax.random.uniform(arg_keys[3], (NLAT,), jnp.float32, math.log(0.3), math.log(3.0))), 0.3, 3.0),
        "spectral_filter": bell_draw(arg_keys[4], (2, L, C), 1.0, 6.0, (), jnp.float32),
        "disco_kernel": bell_draw(arg_keys[5], (NLAT, TAPS, K), TAPS ** -0.5, 2.0, (), jnp.float32),
        "disco_weight": bell_draw(arg_keys[6], (C, K, C), (K * C) ** -0.5, 0.1875),
    }


highest = lax.Precision.HIGHEST


def make_trig(mode_count, point_count):
    wavenumber = lax.broadcasted_iota(jnp.int32, (point_count, mode_count), 1)
    position = lax.broadcasted_iota(jnp.int32, (point_count, mode_count), 0)
    angles = ((wavenumber * position) % point_count).astype(jnp.float32) * (2.0 * jnp.pi / point_count)
    scaled = jnp.stack([jnp.cos(angles), -jnp.sin(angles)], axis=2) * (point_count ** -0.5)
    return scaled.reshape(point_count, 2 * mode_count)


def tap_products(source_field, kernel_rows, disco_weight):
    row_count, lon_count, channels = source_field.shape
    kernel_kinds = disco_weight.shape[1]
    mixtures = jnp.dot(source_field.reshape(row_count * lon_count, channels),
                       disco_weight.reshape(channels, kernel_kinds * channels),
                       preferred_element_type=jnp.float32)
    mixtures = mixtures.reshape(row_count, lon_count, kernel_kinds, channels)
    return jnp.einsum('rnkc,rtk->rntc', mixtures, kernel_rows, precision=highest).astype(jnp.bfloat16)


def reference(grad_output, band_rows, legendre, quad_weights, spectral_filter, disco_kernel, disco_weight):
    slot_ids = jnp.arange(NLAT, dtype=jnp.int32)
    slot_band = slot_ids // ROWS_DEV
    slot_level = slot_ids % ROWS_DEV
    band_start = (jnp.cumsum(band_rows) - band_rows).astype(jnp.int32)
    live_slot = slot_level < band_rows[slot_band]
    global_row = (band_start[slot_band] + slot_level).astype(jnp.int32)
    masked = jnp.where(live_slot[:, None, None], grad_output, jnp.zeros_like(grad_output))
    trig_table = make_trig(M, NLON)

    def forward_band(band_block):
        spectra = jnp.einsum('snc,nk->skc', band_block.astype(jnp.float32), trig_table, precision=highest)
        return spectra.astype(jnp.bfloat16)

    spectra = lax.map(forward_band, masked.reshape(N_LAT, ROWS_DEV, NLON, C)).reshape(NLAT, M, 2, C)
    coefficients = jnp.einsum('mls,smpc->lmpc', legendre, spectra.astype(jnp.float32), precision=highest)
    filter_real = spectral_filter[0][:, None, :]
    filter_imag = spectral_filter[1][:, None, :]
    real_part = coefficients[:, :, 0, :]
    imag_part = coefficients[:, :, 1, :]
    filtered = jnp.stack([filter_real * real_part + filter_imag * imag_part,
                          filter_real * imag_part - filter_imag * real_part], axis=2)
    returned = jnp.einsum('mls,lmpc->smpc', legendre, filtered, precision=highest)
    returned = (returned * quad_weights[:, None, None, None]).astype(jnp.bfloat16)

    def inverse_band(band_block):
        flat_modes = band_block.reshape(ROWS_DEV, 2 * M, C).astype(jnp.float32)
        return jnp.einsum('skc,nk->snc', flat_modes, trig_table, precision=highest).astype(jnp.bfloat16)

    spectral = lax.map(inverse_band, returned.reshape(N_LAT, ROWS_DEV, M, 2, C)).reshape(NLAT, NLON, C)

    block_rows = 32
    block_count = (LIVE + block_rows - 1) // block_rows
    pad_total = block_count * block_rows + 2
    target = jnp.where(live_slot, global_row + 1, pad_total).astype(jnp.int32)
    padded_field = jnp.zeros((pad_total, NLON, C), jnp.bfloat16).at[target].set(masked, mode="drop")
    padded_kernel = jnp.zeros((pad_total, TAPS, K), jnp.float32).at[target].set(disco_kernel, mode="drop")

    def disco_block(start):
        field_rows = lax.dynamic_slice_in_dim(padded_field, start, block_rows + 2, 0)
        kernel_rows = lax.dynamic_slice_in_dim(padded_kernel, start, block_rows + 2, 0)
        products = tap_products(field_rows, kernel_rows, disco_weight).astype(jnp.float32)
        summed = jnp.zeros((block_rows, NLON, C), jnp.float32)
        for row_step in (1, 0, -1):
            source = products[1 - row_step:1 - row_step + block_rows]
            for col_step in (-1, 0, 1):
                tap_index = 3 * (row_step + 1) + col_step + 1
                summed = summed + jnp.roll(source[:, :, tap_index, :], col_step, axis=1)
        return summed

    starts = jnp.arange(block_count, dtype=jnp.int32) * block_rows
    disco_term = lax.map(disco_block, starts).reshape(block_count * block_rows, NLON, C)
    disco_slots = disco_term[jnp.clip(global_row, 0, LIVE - 1)]
    summed = masked.astype(jnp.float32) + disco_slots + spectral.astype(jnp.float32)
    return jnp.where(live_slot[:, None, None], summed, 0.0).astype(jnp.bfloat16)
```

```python
import jax
import jax.numpy as jnp
import ml_dtypes
import numpy as np
from jax import lax
from jax.experimental import pallas as pl
from jax.experimental.pallas import tpu as pltpu
from jax.sharding import PartitionSpec as P

MESH = pl.DeviceIdType.MESH
BF16 = jnp.bfloat16
F32 = jnp.float32

ROWS = 8
LON = 180
LONP = 192
CH = 128
LON_DEV = 8
LAT_DEV = 96
SHARE = CH // LON_DEV
MODES = 192
COEF = 2 * MODES
DEG = 360
DEGP = 384
SLOTS = LAT_DEV * ROWS
TAPS = 9
KINDS = 9
EDGE = 8


def trig_tables():
    points = LON * LON_DEV
    position = np.arange(points)[:, None]
    wavenumber = np.arange(MODES)[None, :]
    angle = (wavenumber * position % points) * (2.0 * np.pi / points)
    table = np.stack([np.cos(angle), -np.sin(angle)], axis=2) * points**-0.5
    blocks = np.zeros((LON_DEV, LONP, COEF))
    blocks[:, :LON] = table.reshape(LON_DEV, LON, COEF)
    inverse = blocks.astype(ml_dtypes.bfloat16)
    forward = np.ascontiguousarray(inverse.reshape(LON_DEV * LONP, COEF).T)
    return forward, inverse


def exchange_groups(rows, group_bit):
    rows = list(rows)
    for half in (4, 2, 1):
        low = (group_bit & half) == 0
        for r in range(ROWS):
            if r & half:
                continue
            a, b = rows[r], rows[r + half]
            rows[r] = jnp.where(low, a, pltpu.roll(b, SHARE * half, 1))
            rows[r + half] = jnp.where(low, pltpu.roll(a, CH - SHARE * half, 1), b)
    return rows


def kernel(
    rows_ref, g_ref, leg_ref, qw_ref, filt_ref, kern_ref, w_ref, tf_ref, ti_ref, out_ref,
    gv, xf, ext, send1, recv1, lat_s1, lat_r1, lat_s2, lat_r2, send2, recv2,
    row_s, row_r, cell_s, cell_r,
    legv, legb, legt, qwv, filtv, filtr, kernv, kpad, kbc, wv, wf, weff,
    tfv, tiv, dsum, coltmp, rhs, zed, pick, outf,
    load_sem, own_sem, s1, r1, s2, r2, hs, hr, ls, lr,
):
    a = lax.axis_index("lat")
    d = lax.axis_index("lon")
    up, down = lax.rem(a + LAT_DEV - 1, LAT_DEV), lax.rem(a + 1, LAT_DEV)
    west, east = lax.rem(d + LON_DEV - 1, LON_DEV), lax.rem(d + 1, LON_DEV)

    def load(i, src, dst):
        copy = pltpu.make_async_copy(src, dst, load_sem.at[i])
        copy.start()
        return copy

    load_g = load(0, g_ref, gv)
    load_leg = load(1, leg_ref, legv)
    load_qw = load(2, qw_ref, qwv)
    load_filt = load(3, filt_ref, filtv)
    load_kern = load(4, kern_ref, kernv)
    load_w = load(5, w_ref, wv)
    load_tf = load(6, tf_ref, tfv)
    load_ti = load(7, ti_ref, tiv)

    barrier = pltpu.get_barrier_semaphore()

    def greet(k, carry):
        pl.semaphore_signal(
            barrier, inc=1, device_id=(lax.rem(a + k, LAT_DEV), d), device_id_type=MESH
        )
        return carry

    lax.fori_loop(1, LAT_DEV, greet, 0)
    for k in range(1, LON_DEV):
        pl.semaphore_signal(
            barrier, inc=1, device_id=(a, lax.rem(d + k, LON_DEV)), device_id_type=MESH
        )
    for lat in (up, down):
        for lon in (west, east):
            pl.semaphore_signal(barrier, inc=1, device_id=(lat, lon), device_id_type=MESH)

    live = rows_ref[a]
    load_g.wait()
    slot3 = lax.broadcasted_iota(jnp.int32, (LON, ROWS, CH), 1)
    masked = jnp.where(slot3 < live, gv[...].astype(F32), 0.0)
    xf[pl.ds(0, LON * ROWS), :] = masked.reshape(LON * ROWS, CH)
    xf[pl.ds(LON * ROWS, (LONP - LON) * ROWS), :] = jnp.zeros(((LONP - LON) * ROWS, CH), F32)
    group16 = lax.broadcasted_iota(jnp.int32, (16, CH), 1) // SHARE

    def spread(chunk, carry):
        first = pl.multiple_of(chunk * 16, 16)
        rows = [xf[pl.ds(first * ROWS + r, 16, stride=ROWS), :] for r in range(ROWS)]
        last_row = jnp.zeros((16, CH), F32)
        for r in range(ROWS):
            ext[r + 1, pl.ds(first + EDGE, 16), :] = rows[r]
            last_row = jnp.where(live == r + 1, rows[r], last_row)
        row_s[0, pl.ds(first, 16), :] = last_row.astype(BF16)
        row_s[1, pl.ds(first, 16), :] = rows[0].astype(BF16)
        swapped = exchange_groups(rows, group16)
        for p in range(LON_DEV):
            send1[p, pl.ds(first, 16), :] = swapped[p].astype(BF16)
        return carry

    lax.fori_loop(0, LONP // 16, spread, 0)

    pl.semaphore_wait(barrier, LAT_DEV - 1 + LON_DEV - 1 + 4)

    def partner(k):
        z, core = d // 2, lax.rem(d, 2)
        return lax.rem(z + k // 2, 4) * 2 + lax.rem(core + k % 2, 2)

    far_first = (4, 5, 2, 6, 3, 7, 1)

    def swap1(k):
        p = partner(k)
        return pltpu.make_async_remote_copy(
            src_ref=send1.at[p], dst_ref=recv1.at[d], send_sem=s1.at[k], recv_sem=r1.at[k],
            device_id=(a, p), device_id_type=MESH,
        )

    for k in far_first:
        swap1(k).start()
    own1 = pltpu.make_async_copy(send1.at[d], recv1.at[d], own_sem.at[0])
    own1.start()

    first_col = xf[pl.ds(0, ROWS), :]
    last_col = xf[pl.ds((LON - 1) * ROWS, ROWS), :]
    slot8 = lax.broadcasted_iota(jnp.int32, (ROWS, CH), 0)
    pad8 = jnp.zeros((ROWS, CH), F32)

    def cell_of(column, slot):
        cell = jnp.sum(jnp.where(slot8 == slot, column, 0.0), axis=0, keepdims=True)
        return jnp.broadcast_to(cell, (16, CH))

    cell_s[0] = jnp.concatenate([last_col, pad8], axis=0).astype(BF16)
    cell_s[1] = jnp.concatenate([first_col, pad8], axis=0).astype(BF16)
    cell_s[2] = cell_of(last_col, live - 1).astype(BF16)
    cell_s[3] = cell_of(first_col, live - 1).astype(BF16)
    cell_s[4] = cell_of(last_col, 0).astype(BF16)
    cell_s[5] = cell_of(first_col, 0).astype(BF16)
    targets = ((a, east), (a, west), (down, east), (down, west), (up, east), (up, west))
    edges = [
        pltpu.make_async_remote_copy(
            src_ref=cell_s.at[i], dst_ref=cell_r.at[i], send_sem=hs.at[i], recv_sem=hr.at[i],
            device_id=target, device_id_type=MESH,
        )
        for i, target in enumerate(targets)
    ] + [
        pltpu.make_async_remote_copy(
            src_ref=row_s.at[i], dst_ref=row_r.at[i], send_sem=hs.at[6 + i], recv_sem=hr.at[6 + i],
            device_id=(lat, d), device_id_type=MESH,
        )
        for i, lat in enumerate((down, up))
    ]
    for copy in edges:
        copy.start()

    load_leg.wait()
    load_qw.wait()
    legb[...] = jnp.zeros_like(legb)
    for mm in range(2):
        legb[mm, pl.ds(0, DEG), :] = legv[mm].astype(BF16)
    zero_rows = jnp.zeros((DEGP - DEG, CH), F32)

    for mm in range(2):
        for block in range(SLOTS // CH):
            at = block * CH
            tile = legv[mm, :, pl.ds(at, CH)] * qwv[:, pl.ds(at, CH)]
            tile = jnp.concatenate([tile, zero_rows], axis=0)
            legt[mm, pl.ds(at, CH), :] = tile.T.astype(BF16)

    load_filt.wait()
    lane = lax.broadcasted_iota(jnp.int32, (DEG, CH), 1)
    filtr[...] = jnp.zeros_like(filtr)
    for part in range(2):
        mine = pltpu.roll(filtv[part], lax.rem(CH - SHARE * d, CH), 1)
        mine = jnp.where(lane < SHARE, mine, 0.0)
        for step in (SHARE, 2 * SHARE, 4 * SHARE):
            mine = mine + pltpu.roll(mine, step, 1)
        filtr[part, pl.ds(0, DEG), :] = mine

    band_row = lax.broadcasted_iota(jnp.int32, (LAT_DEV, SLOTS), 0)
    band_col = lax.broadcasted_iota(jnp.int32, (LAT_DEV, SLOTS), 1) // ROWS
    pick[...] = jnp.where(band_row == band_col, 1.0, 0.0).astype(BF16)

    load_kern.wait()
    kpad[...] = jnp.zeros_like(kpad)
    for t in range(TAPS):
        kpad[pl.ds(16 * t, KINDS), :] = kernv[t]
    above_slot = up * ROWS + rows_ref[up] - 1
    here = lax.broadcasted_iota(jnp.int32, (SLOTS, CH), 1)
    slot_row = lax.broadcasted_iota(jnp.int32, (SLOTS, CH), 0)
    source = jnp.where(here - 1 < live, a * ROWS + here - 1, down * ROWS)
    source = jnp.where(here == 0, above_slot, source)
    one_hot = jnp.where(slot_row == source, 1.0, 0.0)
    chosen = jnp.dot(kpad[...], one_hot, precision=lax.Precision.HIGHEST, preferred_element_type=F32)
    for row in range(ROWS + 2):
        kbc[row] = jnp.broadcast_to(chosen[:, row : row + 1], (16 * TAPS, CH))

    load_w.wait()
    wf[...] = wv[...].astype(F32)

    def weights(step, carry):
        row, half = step // 2, lax.rem(step, 2)
        o = pl.multiple_of(half * 64, 64)
        for t in range(TAPS):
            total = None
            for k in range(KINDS):
                part = wf[k, pl.ds(o, 64), :] * kbc[row, pl.ds(16 * t + k, 1), :]
                total = part if total is None else total + part
            tap_row, tap_col = t // 3, t % 3
            weff[row, pl.ds(tap_col * CH + o, 64), pl.ds(tap_row * CH, CH)] = total.astype(BF16)
        return carry

    lax.fori_loop(0, 2 * (ROWS + 2), weights, 0)

    for copy in edges:
        copy.wait()
    has_above = a > 0
    has_below = a < LAT_DEV - 1
    above_row = jnp.where(has_above, row_r[0].astype(F32), 0.0)
    below_row = jnp.where(has_below, row_r[1].astype(F32), 0.0)
    ext[0, pl.ds(EDGE, LONP), :] = above_row
    for slot in range(1, ROWS):
        old = ext[slot + 1, pl.ds(EDGE, LONP), :]
        ext[slot + 1, pl.ds(EDGE, LONP), :] = jnp.where(live == slot, below_row, old)
    ext[ROWS + 1, pl.ds(EDGE, LONP), :] = jnp.where(live == ROWS, below_row, 0.0)
    for side, at in ((0, EDGE - 1), (1, EDGE + LON)):
        slots = cell_r[side].astype(F32)
        above_cell = jnp.where(has_above, cell_r[2 + side].astype(F32), 0.0)
        below_cell = jnp.where(has_below, cell_r[4 + side].astype(F32), 0.0)
        ext[0, pl.ds(at, 1), :] = above_cell[0:1]
        for slot in range(ROWS + 1):
            edge_cell = jnp.where(live == slot, below_cell[0:1], slots[slot : slot + 1])
            ext[slot + 1, pl.ds(at, 1), :] = edge_cell

    dsum[...] = jnp.zeros_like(dsum)
    for slot in range(ROWS):
        dsum[slot + 2] = xf[pl.ds(slot, LONP, stride=ROWS), :]

    def stencil(row, carry):
        field = jnp.concatenate(
            [ext[row, pl.ds(EDGE - b, LONP), :] for b in (-1, 0, 1)], axis=1
        ).astype(BF16)
        taps = jnp.dot(field, weff[row], preferred_element_type=F32)
        for step in (-1, 0, 1):
            index = (step + 1) * CH
            dsum[row + step + 1] += taps[:, index : index + CH]
        return carry

    lax.fori_loop(0, ROWS + 2, stencil, 0)

    own1.wait()
    for k in far_first:
        swap1(k).wait()
    load_tf.wait()
    spectra = jnp.dot(
        tfv[...], recv1[...].reshape(LON_DEV * LONP, CH), preferred_element_type=F32
    )
    lat_s1[...] = spectra.astype(BF16).reshape(LAT_DEV, 4, CH)

    def all_lat(sent, got, which):
        own = pltpu.make_async_copy(sent.at[a], got.at[a], lr.at[which])
        own.start()

        def send(k, carry):
            j = lax.rem(a + k, LAT_DEV)
            pltpu.make_async_remote_copy(
                src_ref=sent.at[j], dst_ref=got.at[a], send_sem=ls.at[which],
                recv_sem=lr.at[which], device_id=(j, d), device_id_type=MESH,
            ).start()
            return carry

        lax.fori_loop(1, LAT_DEV, send, 0)
        pltpu.make_async_copy(sent, got, lr.at[which]).wait()

    all_lat(lat_s1, lat_r1, 0)

    coltmp[...] = lat_r1[...].astype(F32).reshape(COEF, CH)
    block_slot = lax.broadcasted_iota(jnp.int32, (LAT_DEV, ROWS, CH), 1)
    block_group = lax.broadcasted_iota(jnp.int32, (LAT_DEV, ROWS, CH), 2) // SHARE
    diagonal = block_slot == block_group
    for q in range(4):
        column = coltmp[pl.ds(q, LAT_DEV, stride=4), :]
        wide = jnp.where(diagonal, column[:, None, :], 0.0)
        rhs[:, pl.ds(q * CH, CH)] = wide.reshape(SLOTS, CH).astype(BF16)
    for mm in range(2):
        coef = jnp.dot(legb[mm], rhs[:, pl.ds(mm * 2 * CH, 2 * CH)], preferred_element_type=F32)
        parts = []
        for part in range(2):
            folded = coef[:, part * CH : (part + 1) * CH]
            for step in (SHARE, 2 * SHARE, 4 * SHARE):
                folded = folded + pltpu.roll(folded, step, 1)
            parts.append(folded)
        real, imag = parts
        fr, fi = filtr[0], filtr[1]
        filtered = jnp.concatenate([fr * real + fi * imag, fr * imag - fi * real], axis=1)
        back = jnp.dot(legt[mm], filtered.astype(BF16), preferred_element_type=F32)
        for part in range(2):
            wide = back[:, part * CH : (part + 1) * CH].reshape(LAT_DEV, ROWS, CH)
            wide = jnp.where(diagonal, wide, 0.0).astype(BF16)
            zed[:, pl.ds((2 * mm + part) * CH, CH)] = wide.reshape(SLOTS, CH)
    returned = jnp.dot(pick[...], zed[...], preferred_element_type=F32)
    for q in range(4):
        coltmp[pl.ds(q, LAT_DEV, stride=4), :] = returned[:, q * CH : (q + 1) * CH]
    lat_s2[...] = coltmp[...].astype(BF16).reshape(LAT_DEV, 4, CH)
    all_lat(lat_s2, lat_r2, 1)

    load_ti.wait()
    modes = lat_r2[...].reshape(COEF, CH)

    def block_of(p):
        send2[p] = jnp.dot(tiv[p], modes, preferred_element_type=F32).astype(BF16)

    def swap2(k):
        p = partner(k)
        return pltpu.make_async_remote_copy(
            src_ref=send2.at[p], dst_ref=recv2.at[d], send_sem=s2.at[k], recv_sem=r2.at[k],
            device_id=(a, p), device_id_type=MESH,
        )

    for k in far_first:
        block_of(partner(k))
        swap2(k).start()
    block_of(d)
    own2 = pltpu.make_async_copy(send2.at[d], recv2.at[d], own_sem.at[1])
    own2.start()
    own2.wait()
    for k in far_first:
        swap2(k).wait()

    def gather(chunk, carry):
        first = pl.multiple_of(chunk * 16, 16)
        blocks = [recv2[e, pl.ds(first, 16), :].astype(F32) for e in range(LON_DEV)]
        rows = exchange_groups(blocks, group16)
        for r in range(ROWS):
            total = dsum[r + 2, pl.ds(first, 16), :] + rows[r]
            outf[pl.ds(first * ROWS + r, 16, stride=ROWS), :] = jnp.where(r < live, total, 0.0)
        return carry

    lax.fori_loop(0, LONP // 16, gather, 0)
    out_ref[...] = outf[pl.ds(0, LON * ROWS), :].astype(BF16).reshape(LON, ROWS, CH)

    for which, sent in ((0, lat_s1), (1, lat_s2)):
        most = sent.at[pl.ds(0, LAT_DEV - 1)]
        pltpu.make_async_copy(most, most, ls.at[which]).wait()


def on_device(grad_output, band_rows, legendre, quad_weights, spectral_filter, disco_kernel, disco_weight):
    forward, inverse = trig_tables()
    any_space = pl.BlockSpec(memory_space=pl.ANY)
    vmem = pltpu.VMEM
    dma = pltpu.SemaphoreType.DMA
    out = pl.pallas_call(
        kernel,
        out_shape=jax.ShapeDtypeStruct((LON, ROWS, CH), BF16),
        in_specs=[pl.BlockSpec(memory_space=pltpu.SMEM)] + [any_space] * 8,
        out_specs=pl.BlockSpec(memory_space=pltpu.VMEM),
        scratch_shapes=[
            vmem((LON, ROWS, CH), BF16),
            vmem((LONP * ROWS, CH), F32),
            vmem((ROWS + 2, LONP + 2 * EDGE, CH), F32),
            vmem((LON_DEV, LONP, CH), BF16),
            vmem((LON_DEV, LONP, CH), BF16),
            vmem((LAT_DEV, 4, CH), BF16),
            vmem((LAT_DEV, 4, CH), BF16),
            vmem((LAT_DEV, 4, CH), BF16),
            vmem((LAT_DEV, 4, CH), BF16),
            vmem((LON_DEV, LONP, CH), BF16),
            vmem((LON_DEV, LONP, CH), BF16),
            vmem((2, LONP, CH), BF16),
            vmem((2, LONP, CH), BF16),
            vmem((6, 16, CH), BF16),
            vmem((6, 16, CH), BF16),
            vmem((2, DEG, SLOTS), F32),
            vmem((2, DEGP, SLOTS), BF16),
            vmem((2, SLOTS, DEGP), BF16),
            vmem((1, SLOTS), F32),
            vmem((2, DEG, CH), F32),
            vmem((2, DEGP, CH), F32),
            vmem((TAPS, KINDS, SLOTS), F32),
            vmem((16 * TAPS, SLOTS), F32),
            vmem((ROWS + 2, 16 * TAPS, CH), F32),
            vmem((KINDS, CH, CH), BF16),
            vmem((KINDS, CH, CH), F32),
            vmem((ROWS + 2, 3 * CH, 3 * CH), BF16),
            vmem((COEF, LON_DEV * LONP), BF16),
            vmem((LON_DEV, LONP, COEF), BF16),
            vmem((ROWS + 4, LONP, CH), F32),
            vmem((COEF, CH), F32),
            vmem((SLOTS, 4 * CH), BF16),
            vmem((SLOTS, 4 * CH), BF16),
            vmem((LAT_DEV, SLOTS), BF16),
            vmem((LONP * ROWS, CH), F32),
            dma((8,)),
            dma((2,)),
            dma((8,)),
            dma((8,)),
            dma((8,)),
            dma((8,)),
            dma((8,)),
            dma((8,)),
            dma((2,)),
            dma((2,)),
        ],
        compiler_params=pltpu.CompilerParams(
            collective_id=0, has_side_effects=True, vmem_limit_bytes=56 * 2**20
        ),
    )(
        band_rows,
        jnp.transpose(grad_output, (1, 0, 2)),
        legendre,
        quad_weights.reshape(1, SLOTS),
        spectral_filter,
        jnp.transpose(disco_kernel, (1, 2, 0)),
        jnp.transpose(disco_weight, (1, 0, 2)),
        jnp.asarray(forward),
        jnp.asarray(inverse),
    )
    return jnp.transpose(out, (1, 0, 2))


def solution(mesh):
    placed = (P("lat", "lon", None), P(), P("lat", None, None), P(), P(), P(), P())
    return jax.shard_map(
        on_device, mesh=mesh, in_specs=placed, out_specs=P("lat", "lon", None), check_vma=False
    )
```

```python
import jax
import jax.numpy as jnp
import ml_dtypes
import numpy as np
from jax import lax
from jax.experimental import pallas as pl
from jax.experimental.pallas import tpu as pltpu
from jax.sharding import PartitionSpec as P

MESH = pl.DeviceIdType.MESH
BF16 = jnp.bfloat16
F32 = jnp.float32

ROWS = 8
LON = 180
LONP = 192
CH = 128
LON_DEV = 8
LAT_DEV = 96
SHARE = CH // LON_DEV
MODES = 192
COEF = 2 * MODES
DEG = 360
DEGP = 384
SLOTS = LAT_DEV * ROWS
TAPS = 9
KINDS = 9
EDGE = 8


def trig_tables():
    points = LON * LON_DEV
    position = np.arange(points)[:, None]
    wavenumber = np.arange(MODES)[None, :]
    angle = (wavenumber * position % points) * (2.0 * np.pi / points)
    table = np.stack([np.cos(angle), -np.sin(angle)], axis=2) * points**-0.5
    blocks = np.zeros((LON_DEV, LONP, COEF))
    blocks[:, :LON] = table.reshape(LON_DEV, LON, COEF)
    inverse = blocks.astype(ml_dtypes.bfloat16)
    forward = np.ascontiguousarray(inverse.reshape(LON_DEV * LONP, COEF).T)
    return forward, inverse


def exchange_groups(rows, group_bit):
    rows = list(rows)
    for half in (4, 2, 1):
        low = (group_bit & half) == 0
        for r in range(ROWS):
            if r & half:
                continue
            a, b = rows[r], rows[r + half]
            rows[r] = jnp.where(low, a, pltpu.roll(b, SHARE * half, 1))
            rows[r + half] = jnp.where(low, pltpu.roll(a, CH - SHARE * half, 1), b)
    return rows


def kernel(
    rows_ref, qw_ref, g_ref, leg_ref, filt_ref, kern_ref, w_ref, tf_ref, ti_ref, out_ref,
    gv, xf, ext, send1, recv1, lat_s1, lat_r1, lat_s2, lat_r2, send2, recv2,
    row_s, row_r, cell_s, cell_r,
    legv, legb, legt, filtv, filtr, kernv, kpad, kbc, wv, wf, weff,
    tfv, tiv, dsum, coltmp, rhs, zed, pick, outf,
    load_sem, own_sem, s1, r1, s2, r2, hs, hr, ls, lr,
):
    a = lax.axis_index("lat")
    d = lax.axis_index("lon")
    up, down = lax.rem(a + LAT_DEV - 1, LAT_DEV), lax.rem(a + 1, LAT_DEV)
    west, east = lax.rem(d + LON_DEV - 1, LON_DEV), lax.rem(d + 1, LON_DEV)

    def load(i, src, dst):
        copy = pltpu.make_async_copy(src, dst, load_sem.at[i])
        copy.start()
        return copy

    load_g = load(0, g_ref, gv)

    barrier = pltpu.get_barrier_semaphore()

    def lat_after(k):
        j = a + k
        return jnp.where(j >= LAT_DEV, j - LAT_DEV, j)

    def greet(k, carry):
        pl.semaphore_signal(barrier, inc=1, device_id=(lat_after(k), d), device_id_type=MESH)
        return carry

    lax.fori_loop(1, LAT_DEV, greet, 0, unroll=5)
    for k in range(1, LON_DEV):
        pl.semaphore_signal(
            barrier, inc=1, device_id=(a, lax.rem(d + k, LON_DEV)), device_id_type=MESH
        )
    for lat in (up, down):
        for lon in (west, east):
            pl.semaphore_signal(barrier, inc=1, device_id=(lat, lon), device_id_type=MESH)
    load_leg = load(1, leg_ref, legv)
    load_filt = load(2, filt_ref, filtv)
    load_kern = load(3, kern_ref, kernv)
    load_w = load(4, w_ref, wv)
    load_tf = load(5, tf_ref, tfv)
    load_ti = load(6, ti_ref, tiv)

    live = rows_ref[a]
    load_g.wait()
    slot3 = lax.broadcasted_iota(jnp.int32, (LON, ROWS, CH), 1)
    masked = jnp.where(slot3 < live, gv[...].astype(F32), 0.0)
    xf[pl.ds(0, LON * ROWS), :] = masked.reshape(LON * ROWS, CH)
    xf[pl.ds(LON * ROWS, (LONP - LON) * ROWS), :] = jnp.zeros(((LONP - LON) * ROWS, CH), F32)
    group16 = lax.broadcasted_iota(jnp.int32, (16, CH), 1) // SHARE

    for chunk in range(LONP // 16):
        first = chunk * 16
        rows = [xf[pl.ds(first * ROWS + r, 16, stride=ROWS), :] for r in range(ROWS)]
        swapped = exchange_groups(rows, group16)
        for p in range(LON_DEV):
            send1[p, pl.ds(first, 16), :] = swapped[p].astype(BF16)

    pl.semaphore_wait(barrier, LAT_DEV - 1 + LON_DEV - 1 + 4)

    def partner(k):
        z, core = d // 2, lax.rem(d, 2)
        return lax.rem(z + k // 2, 4) * 2 + lax.rem(core + k % 2, 2)

    far_first = (4, 5, 2, 6, 3, 7, 1)

    def swap1(k):
        p = partner(k)
        return pltpu.make_async_remote_copy(
            src_ref=send1.at[p], dst_ref=recv1.at[d], send_sem=s1.at[k], recv_sem=r1.at[k],
            device_id=(a, p), device_id_type=MESH,
        )

    for k in far_first:
        swap1(k).start()
    own1 = pltpu.make_async_copy(send1.at[d], recv1.at[d], own_sem.at[0])
    own1.start()

    for r in range(ROWS):
        row = xf[pl.ds(r, LONP, stride=ROWS), :]
        ext[r + 1, pl.ds(EDGE, LONP), :] = row
        dsum[r + 2] = row
        if r == 0:
            row_s[1] = row.astype(BF16)
            last_row = row
        else:
            last_row = jnp.where(live == r + 1, row, last_row)
    row_s[0] = last_row.astype(BF16)
    first_col = xf[pl.ds(0, ROWS), :]
    last_col = xf[pl.ds((LON - 1) * ROWS, ROWS), :]
    slot8 = lax.broadcasted_iota(jnp.int32, (ROWS, CH), 0)
    pad8 = jnp.zeros((ROWS, CH), F32)

    def cell_of(column, slot):
        cell = jnp.sum(jnp.where(slot8 == slot, column, 0.0), axis=0, keepdims=True)
        return jnp.broadcast_to(cell, (16, CH))

    cell_s[0] = jnp.concatenate([last_col, pad8], axis=0).astype(BF16)
    cell_s[1] = jnp.concatenate([first_col, pad8], axis=0).astype(BF16)
    cell_s[2] = cell_of(last_col, live - 1).astype(BF16)
    cell_s[3] = cell_of(first_col, live - 1).astype(BF16)
    cell_s[4] = cell_of(last_col, 0).astype(BF16)
    cell_s[5] = cell_of(first_col, 0).astype(BF16)
    targets = ((a, east), (a, west), (down, east), (down, west), (up, east), (up, west))
    edges = [
        pltpu.make_async_remote_copy(
            src_ref=cell_s.at[i], dst_ref=cell_r.at[i], send_sem=hs.at[i], recv_sem=hr.at[i],
            device_id=target, device_id_type=MESH,
        )
        for i, target in enumerate(targets)
    ] + [
        pltpu.make_async_remote_copy(
            src_ref=row_s.at[i], dst_ref=row_r.at[i], send_sem=hs.at[6 + i], recv_sem=hr.at[6 + i],
            device_id=(lat, d), device_id_type=MESH,
        )
        for i, lat in enumerate((down, up))
    ]
    for copy in edges:
        copy.start()

    load_leg.wait()
    legb[...] = jnp.zeros_like(legb)
    for mm in range(2):
        legb[mm, pl.ds(0, DEG), :] = legv[mm].astype(BF16)
    zero_rows = jnp.zeros((DEGP - DEG, CH), F32)

    for mm in range(2):
        for block in range(SLOTS // CH):
            at = block * CH
            tile = jnp.concatenate([legv[mm, :, pl.ds(at, CH)], zero_rows], axis=0)
            legt[mm, pl.ds(at, CH), :] = tile.T.astype(BF16)

    load_filt.wait()
    lane = lax.broadcasted_iota(jnp.int32, (DEG, CH), 1)
    filtr[...] = jnp.zeros_like(filtr)
    for part in range(2):
        mine = pltpu.roll(filtv[part], lax.rem(CH - SHARE * d, CH), 1)
        mine = jnp.where(lane < SHARE, mine, 0.0)
        for step in (SHARE, 2 * SHARE, 4 * SHARE):
            mine = mine + pltpu.roll(mine, step, 1)
        filtr[part, pl.ds(0, DEG), :] = mine

    band_row = lax.broadcasted_iota(jnp.int32, (LAT_DEV, SLOTS), 0)
    band_col = lax.broadcasted_iota(jnp.int32, (LAT_DEV, SLOTS), 1) // ROWS
    pick[...] = jnp.where(band_row == band_col, 1.0, 0.0).astype(BF16)

    load_kern.wait()
    kpad[...] = jnp.zeros_like(kpad)
    for t in range(TAPS):
        kpad[pl.ds(16 * t, KINDS), :] = kernv[t]
    above_slot = up * ROWS + rows_ref[up] - 1
    here = lax.broadcasted_iota(jnp.int32, (SLOTS, CH), 1)
    slot_row = lax.broadcasted_iota(jnp.int32, (SLOTS, CH), 0)
    source = jnp.where(here - 1 < live, a * ROWS + here - 1, down * ROWS)
    source = jnp.where(here == 0, above_slot, source)
    one_hot = jnp.where(slot_row == source, 1.0, 0.0)
    chosen = jnp.dot(kpad[...], one_hot, precision=lax.Precision.HIGHEST, preferred_element_type=F32)
    for row in range(ROWS + 2):
        kbc[row] = jnp.broadcast_to(chosen[:, row : row + 1], (16 * TAPS, CH))

    load_w.wait()
    wf[...] = wv[...].astype(F32)

    def weights(step, carry):
        row, half = step // 2, lax.rem(step, 2)
        o = pl.multiple_of(half * 64, 64)
        for t in range(TAPS):
            total = None
            for k in range(KINDS):
                part = wf[k, pl.ds(o, 64), :] * kbc[row, pl.ds(16 * t + k, 1), :]
                total = part if total is None else total + part
            tap_row, tap_col = t // 3, t % 3
            weff[row, pl.ds(tap_col * CH + o, 64), pl.ds(tap_row * CH, CH)] = total.astype(BF16)
        return carry

    lax.fori_loop(0, 2 * (ROWS + 2), weights, 0)

    own1.wait()
    for k in far_first:
        swap1(k).wait()
    load_tf.wait()
    spectra = jnp.dot(
        tfv[...], recv1[...].reshape(LON_DEV * LONP, CH), preferred_element_type=F32
    )
    lat_s1[...] = spectra.astype(BF16).reshape(LAT_DEV, 4, CH)

    def all_lat(sent, got, which):
        own = pltpu.make_async_copy(sent.at[a], got.at[a], lr.at[which])
        own.start()

        def send(k, carry):
            j = lat_after(k)
            pltpu.make_async_remote_copy(
                src_ref=sent.at[j], dst_ref=got.at[a], send_sem=ls.at[which],
                recv_sem=lr.at[which], device_id=(j, d), device_id_type=MESH,
            ).start()
            return carry

        lax.fori_loop(1, LAT_DEV, send, 0, unroll=5)
        pltpu.make_async_copy(sent, got, lr.at[which]).wait()

    all_lat(lat_s1, lat_r1, 0)

    coltmp[...] = lat_r1[...].astype(F32).reshape(COEF, CH)
    block_slot = lax.broadcasted_iota(jnp.int32, (LAT_DEV, ROWS, CH), 1)
    block_group = lax.broadcasted_iota(jnp.int32, (LAT_DEV, ROWS, CH), 2) // SHARE
    diagonal = block_slot == block_group
    for q in range(4):
        column = coltmp[pl.ds(q, LAT_DEV, stride=4), :]
        wide = jnp.where(diagonal, column[:, None, :], 0.0)
        rhs[:, pl.ds(q * CH, CH)] = wide.reshape(SLOTS, CH).astype(BF16)
    for mm in range(2):
        coef = jnp.dot(legb[mm], rhs[:, pl.ds(mm * 2 * CH, 2 * CH)], preferred_element_type=F32)
        parts = []
        for part in range(2):
            folded = coef[:, part * CH : (part + 1) * CH]
            for step in (SHARE, 2 * SHARE, 4 * SHARE):
                folded = folded + pltpu.roll(folded, step, 1)
            parts.append(folded)
        real, imag = parts
        fr, fi = filtr[0], filtr[1]
        filtered = jnp.concatenate([fr * real + fi * imag, fr * imag - fi * real], axis=1)
        back = jnp.dot(legt[mm], filtered.astype(BF16), preferred_element_type=F32)
        for part in range(2):
            wide = back[:, part * CH : (part + 1) * CH].reshape(LAT_DEV, ROWS, CH)
            wide = jnp.where(diagonal, wide, 0.0).astype(BF16)
            zed[:, pl.ds((2 * mm + part) * CH, CH)] = wide.reshape(SLOTS, CH)
    returned = jnp.dot(pick[...], zed[...], preferred_element_type=F32)
    for q in range(4):
        coltmp[pl.ds(q, LAT_DEV, stride=4), :] = returned[:, q * CH : (q + 1) * CH]
    lat_s2[...] = coltmp[...].astype(BF16).reshape(LAT_DEV, 4, CH)
    all_lat(lat_s2, lat_r2, 1)

    load_ti.wait()
    modes = lat_r2[...].reshape(COEF, CH)

    def block_of(p):
        send2[p] = jnp.dot(tiv[p], modes, preferred_element_type=F32).astype(BF16)

    def swap2(k):
        p = partner(k)
        return pltpu.make_async_remote_copy(
            src_ref=send2.at[p], dst_ref=recv2.at[d], send_sem=s2.at[k], recv_sem=r2.at[k],
            device_id=(a, p), device_id_type=MESH,
        )

    for k in far_first:
        block_of(partner(k))
        swap2(k).start()
    block_of(d)
    own2 = pltpu.make_async_copy(send2.at[d], recv2.at[d], own_sem.at[1])
    own2.start()

    for copy in edges:
        copy.wait()
    has_above = a > 0
    has_below = a < LAT_DEV - 1
    above_row = jnp.where(has_above, row_r[0].astype(F32), 0.0)
    below_row = jnp.where(has_below, row_r[1].astype(F32), 0.0)
    ext[0, pl.ds(EDGE, LONP), :] = above_row
    for slot in range(1, ROWS):
        old = ext[slot + 1, pl.ds(EDGE, LONP), :]
        ext[slot + 1, pl.ds(EDGE, LONP), :] = jnp.where(live == slot, below_row, old)
    ext[ROWS + 1, pl.ds(EDGE, LONP), :] = jnp.where(live == ROWS, below_row, 0.0)
    for side, at in ((0, EDGE - 1), (1, EDGE + LON)):
        slots = cell_r[side].astype(F32)
        above_cell = jnp.where(has_above, cell_r[2 + side].astype(F32), 0.0)
        below_cell = jnp.where(has_below, cell_r[4 + side].astype(F32), 0.0)
        ext[0, pl.ds(at, 1), :] = above_cell[0:1]
        for slot in range(ROWS + 1):
            edge_cell = jnp.where(live == slot, below_cell[0:1], slots[slot : slot + 1])
            ext[slot + 1, pl.ds(at, 1), :] = edge_cell

    for spare in (0, 1, ROWS + 2, ROWS + 3):
        dsum[spare] = jnp.zeros((LONP, CH), F32)

    def stencil(row, carry):
        field = jnp.concatenate(
            [ext[row, pl.ds(EDGE - b, LONP), :] for b in (-1, 0, 1)], axis=1
        ).astype(BF16)
        taps = jnp.dot(field, weff[row], preferred_element_type=F32)
        for step in (-1, 0, 1):
            index = (step + 1) * CH
            dsum[row + step + 1] += taps[:, index : index + CH]
        return carry

    lax.fori_loop(0, ROWS + 2, stencil, 0)

    own2.wait()
    for k in far_first:
        swap2(k).wait()
    for chunk in range(LONP // 16):
        first = chunk * 16
        blocks = [recv2[e, pl.ds(first, 16), :].astype(F32) for e in range(LON_DEV)]
        rows = exchange_groups(blocks, group16)
        for r in range(ROWS):
            total = dsum[r + 2, pl.ds(first, 16), :]
            total = total + rows[r] * qw_ref[a * ROWS + r]
            total = jnp.where(r < live, total, 0.0)
            outf[pl.ds(first * ROWS + r, 16, stride=ROWS), :] = total
    out_ref[...] = outf[pl.ds(0, LON * ROWS), :].astype(BF16).reshape(LON, ROWS, CH)

    for which, sent in ((0, lat_s1), (1, lat_s2)):
        most = sent.at[pl.ds(0, LAT_DEV - 1)]
        pltpu.make_async_copy(most, most, ls.at[which]).wait()


def on_device(grad_output, band_rows, legendre, quad_weights, spectral_filter, disco_kernel, disco_weight):
    forward, inverse = trig_tables()
    any_space = pl.BlockSpec(memory_space=pl.ANY)
    vmem = pltpu.VMEM
    dma = pltpu.SemaphoreType.DMA
    out = pl.pallas_call(
        kernel,
        out_shape=jax.ShapeDtypeStruct((LON, ROWS, CH), BF16),
        in_specs=[pl.BlockSpec(memory_space=pltpu.SMEM)] * 2 + [any_space] * 7,
        out_specs=pl.BlockSpec(memory_space=pltpu.VMEM),
        scratch_shapes=[
            vmem((LON, ROWS, CH), BF16),
            vmem((LONP * ROWS, CH), F32),
            vmem((ROWS + 2, LONP + 2 * EDGE, CH), F32),
            vmem((LON_DEV, LONP, CH), BF16),
            vmem((LON_DEV, LONP, CH), BF16),
            vmem((LAT_DEV, 4, CH), BF16),
            vmem((LAT_DEV, 4, CH), BF16),
            vmem((LAT_DEV, 4, CH), BF16),
            vmem((LAT_DEV, 4, CH), BF16),
            vmem((LON_DEV, LONP, CH), BF16),
            vmem((LON_DEV, LONP, CH), BF16),
            vmem((2, LONP, CH), BF16),
            vmem((2, LONP, CH), BF16),
            vmem((6, 16, CH), BF16),
            vmem((6, 16, CH), BF16),
            vmem((2, DEG, SLOTS), F32),
            vmem((2, DEGP, SLOTS), BF16),
            vmem((2, SLOTS, DEGP), BF16),
            vmem((2, DEG, CH), F32),
            vmem((2, DEGP, CH), F32),
            vmem((TAPS, KINDS, SLOTS), F32),
            vmem((16 * TAPS, SLOTS), F32),
            vmem((ROWS + 2, 16 * TAPS, CH), F32),
            vmem((KINDS, CH, CH), BF16),
            vmem((KINDS, CH, CH), F32),
            vmem((ROWS + 2, 3 * CH, 3 * CH), BF16),
            vmem((COEF, LON_DEV * LONP), BF16),
            vmem((LON_DEV, LONP, COEF), BF16),
            vmem((ROWS + 4, LONP, CH), F32),
            vmem((COEF, CH), F32),
            vmem((SLOTS, 4 * CH), BF16),
            vmem((SLOTS, 4 * CH), BF16),
            vmem((LAT_DEV, SLOTS), BF16),
            vmem((LONP * ROWS, CH), F32),
            dma((8,)),
            dma((2,)),
            dma((8,)),
            dma((8,)),
            dma((8,)),
            dma((8,)),
            dma((8,)),
            dma((8,)),
            dma((2,)),
            dma((2,)),
        ],
        compiler_params=pltpu.CompilerParams(
            collective_id=0, has_side_effects=True, vmem_limit_bytes=56 * 2**20
        ),
    )(
        band_rows,
        quad_weights,
        jnp.transpose(grad_output, (1, 0, 2)),
        legendre,
        spectral_filter,
        jnp.transpose(disco_kernel, (1, 2, 0)),
        jnp.transpose(disco_weight, (1, 0, 2)),
        jnp.asarray(forward),
        jnp.asarray(inverse),
    )
    return jnp.transpose(out, (1, 0, 2))


def solution(mesh):
    placed = (P("lat", "lon", None), P(), P("lat", None, None), P(), P(), P(), P())
    return jax.shard_map(
        on_device, mesh=mesh, in_specs=placed, out_specs=P("lat", "lon", None), check_vma=False
    )
```

```python
import jax
import jax.numpy as jnp
import ml_dtypes
import numpy as np
from jax import lax
from jax.experimental import pallas as pl
from jax.experimental.pallas import tpu as pltpu
from jax.sharding import PartitionSpec as P

MESH = pl.DeviceIdType.MESH
BF16 = jnp.bfloat16
F32 = jnp.float32

ROWS = 8
LON = 180
LONP = 192
HALF = LONP // 2
CH = 128
LON_DEV = 8
LAT_DEV = 96
X_DEV, Y_DEV, Z_DEV = 4, 8, 3
SHARE = CH // LON_DEV
MODES = 192
COEF = 2 * MODES
DEG = 360
DEGP = 384
SLOTS = LAT_DEV * ROWS
TAPS = 9
KINDS = 9
EDGE = 8


def trig_tables():
    points = LON * LON_DEV
    position = np.arange(points)[:, None]
    wavenumber = np.arange(MODES)[None, :]
    angle = (wavenumber * position % points) * (2.0 * np.pi / points)
    table = np.stack([np.cos(angle), -np.sin(angle)], axis=2) * points**-0.5
    blocks = np.zeros((LON_DEV, LONP, COEF))
    blocks[:, :LON] = table.reshape(LON_DEV, LON, COEF)
    inverse = blocks.astype(ml_dtypes.bfloat16)
    forward = np.ascontiguousarray(inverse.reshape(LON_DEV * LONP, COEF).T)
    return forward, inverse


def exchange_groups(rows, group_bit):
    rows = list(rows)
    for half in (4, 2, 1):
        low = (group_bit & half) == 0
        for r in range(ROWS):
            if r & half:
                continue
            a, b = rows[r], rows[r + half]
            rows[r] = jnp.where(low, a, pltpu.roll(b, SHARE * half, 1))
            rows[r + half] = jnp.where(low, pltpu.roll(a, CH - SHARE * half, 1), b)
    return rows


def kernel(
    rows_ref, qw_ref, g_ref, leg_ref, filt_ref, kern_ref, w_ref, tf_ref, ti_ref, out_ref,
    gv, xf, ext, send1, recv1, lat_s1, lat_r1, lat_s2, lat_r2, send2, recv2,
    row_s, row_r, cell_s, cell_r,
    legv, legb, legt, filtv, filtr, kernv, kpad, kbc, wv, wf, weff,
    tfv, tiv, dsum, coltmp, rhs, zed, pick, outf,
    load_sem, own_sem, s1, r1, s2, r2, hs, hr, ls, lr,
):
    a = lax.axis_index("lat")
    d = lax.axis_index("lon")
    up, down = lax.rem(a + LAT_DEV - 1, LAT_DEV), lax.rem(a + 1, LAT_DEV)
    west, east = lax.rem(d + LON_DEV - 1, LON_DEV), lax.rem(d + 1, LON_DEV)

    def load(i, src, dst):
        copy = pltpu.make_async_copy(src, dst, load_sem.at[i])
        copy.start()
        return copy

    load_g = (
        load(0, g_ref.at[pl.ds(0, HALF)], gv.at[pl.ds(0, HALF)]),
        load(7, g_ref.at[pl.ds(HALF, LON - HALF)], gv.at[pl.ds(HALF, LON - HALF)]),
    )

    barrier = pltpu.get_barrier_semaphore()

    def lat_after(k):
        j = a + k
        return jnp.where(j >= LAT_DEV, j - LAT_DEV, j)

    def greet(k, carry):
        pl.semaphore_signal(barrier, inc=1, device_id=(lat_after(k), d), device_id_type=MESH)
        return carry

    lax.fori_loop(1, LAT_DEV, greet, 0, unroll=5)
    for k in range(1, LON_DEV):
        pl.semaphore_signal(
            barrier, inc=1, device_id=(a, lax.rem(d + k, LON_DEV)), device_id_type=MESH
        )
    for lat in (up, down):
        for lon in (west, east):
            pl.semaphore_signal(barrier, inc=1, device_id=(lat, lon), device_id_type=MESH)
    load_leg = load(1, leg_ref, legv)
    load_filt = load(2, filt_ref, filtv)
    load_kern = load(3, kern_ref, kernv)
    load_w = load(4, w_ref, wv)
    load_tf = load(5, tf_ref, tfv)
    load_ti = load(6, ti_ref, tiv)

    live = rows_ref[a]
    group16 = lax.broadcasted_iota(jnp.int32, (16, CH), 1) // SHARE

    def partner(k):
        z, core = d // 2, lax.rem(d, 2)
        return lax.rem(z + k // 2, 4) * 2 + lax.rem(core + k % 2, 2)

    far_first = (4, 5, 2, 6, 3, 7, 1)

    def swap(sent, got, send_sem, recv_sem, half, k):
        p = partner(k)
        part = pl.ds(half * HALF, HALF)
        return pltpu.make_async_remote_copy(
            src_ref=sent.at[p, part], dst_ref=got.at[d, part], send_sem=send_sem.at[half, k],
            recv_sem=recv_sem.at[half, k], device_id=(a, p), device_id_type=MESH,
        )

    for half in range(2):
        load_g[half].wait()
        count = HALF if half == 0 else LON - HALF
        slot3 = lax.broadcasted_iota(jnp.int32, (count, ROWS, CH), 1)
        masked = jnp.where(slot3 < live, gv[pl.ds(half * HALF, count)].astype(F32), 0.0)
        xf[pl.ds(half * HALF * ROWS, count * ROWS), :] = masked.reshape(count * ROWS, CH)
        if half == 1:
            xf[pl.ds(LON * ROWS, (LONP - LON) * ROWS), :] = jnp.zeros(((LONP - LON) * ROWS, CH), F32)
        for chunk in range(HALF // 16):
            first = half * HALF + chunk * 16
            rows = [xf[pl.ds(first * ROWS + r, 16, stride=ROWS), :] for r in range(ROWS)]
            swapped = exchange_groups(rows, group16)
            for p in range(LON_DEV):
                send1[p, pl.ds(first, 16), :] = swapped[p].astype(BF16)
        if half == 0:
            pl.semaphore_wait(barrier, LAT_DEV - 1 + LON_DEV - 1 + 4)
        for k in far_first:
            swap(send1, recv1, s1, r1, half, k).start()
    own1 = pltpu.make_async_copy(send1.at[d], recv1.at[d], own_sem.at[0])
    own1.start()

    for r in range(ROWS):
        row = xf[pl.ds(r, LONP, stride=ROWS), :]
        ext[r + 1, pl.ds(EDGE, LONP), :] = row
        dsum[r + 2] = row
        if r == 0:
            row_s[1] = row.astype(BF16)
            last_row = row
        else:
            last_row = jnp.where(live == r + 1, row, last_row)
    row_s[0] = last_row.astype(BF16)
    first_col = xf[pl.ds(0, ROWS), :]
    last_col = xf[pl.ds((LON - 1) * ROWS, ROWS), :]
    slot8 = lax.broadcasted_iota(jnp.int32, (ROWS, CH), 0)
    pad8 = jnp.zeros((ROWS, CH), F32)

    def cell_of(column, slot):
        cell = jnp.sum(jnp.where(slot8 == slot, column, 0.0), axis=0, keepdims=True)
        return jnp.broadcast_to(cell, (16, CH))

    cell_s[0] = jnp.concatenate([last_col, pad8], axis=0).astype(BF16)
    cell_s[1] = jnp.concatenate([first_col, pad8], axis=0).astype(BF16)
    cell_s[2] = cell_of(last_col, live - 1).astype(BF16)
    cell_s[3] = cell_of(first_col, live - 1).astype(BF16)
    cell_s[4] = cell_of(last_col, 0).astype(BF16)
    cell_s[5] = cell_of(first_col, 0).astype(BF16)
    targets = ((a, east), (a, west), (down, east), (down, west), (up, east), (up, west))
    edges = [
        pltpu.make_async_remote_copy(
            src_ref=cell_s.at[i], dst_ref=cell_r.at[i], send_sem=hs.at[i], recv_sem=hr.at[i],
            device_id=target, device_id_type=MESH,
        )
        for i, target in enumerate(targets)
    ] + [
        pltpu.make_async_remote_copy(
            src_ref=row_s.at[i], dst_ref=row_r.at[i], send_sem=hs.at[6 + i], recv_sem=hr.at[6 + i],
            device_id=(lat, d), device_id_type=MESH,
        )
        for i, lat in enumerate((down, up))
    ]
    for copy in edges:
        copy.start()

    load_leg.wait()
    legb[...] = jnp.zeros_like(legb)
    for mm in range(2):
        legb[mm, pl.ds(0, DEG), :] = legv[mm].astype(BF16)
    zero_rows = jnp.zeros((DEGP - DEG, CH), F32)

    for mm in range(2):
        for block in range(SLOTS // CH):
            at = block * CH
            tile = jnp.concatenate([legv[mm, :, pl.ds(at, CH)], zero_rows], axis=0)
            legt[mm, pl.ds(at, CH), :] = tile.T.astype(BF16)

    load_filt.wait()
    lane = lax.broadcasted_iota(jnp.int32, (DEG, CH), 1)
    filtr[...] = jnp.zeros_like(filtr)
    for part in range(2):
        mine = pltpu.roll(filtv[part], lax.rem(CH - SHARE * d, CH), 1)
        mine = jnp.where(lane < SHARE, mine, 0.0)
        for step in (SHARE, 2 * SHARE, 4 * SHARE):
            mine = mine + pltpu.roll(mine, step, 1)
        filtr[part, pl.ds(0, DEG), :] = mine

    band_row = lax.broadcasted_iota(jnp.int32, (LAT_DEV, SLOTS), 0)
    band_col = lax.broadcasted_iota(jnp.int32, (LAT_DEV, SLOTS), 1) // ROWS
    pick[...] = jnp.where(band_row == band_col, 1.0, 0.0).astype(BF16)

    load_kern.wait()
    kpad[...] = jnp.zeros_like(kpad)
    for t in range(TAPS):
        kpad[pl.ds(16 * t, KINDS), :] = kernv[t]
    above_slot = up * ROWS + rows_ref[up] - 1
    here = lax.broadcasted_iota(jnp.int32, (SLOTS, CH), 1)
    slot_row = lax.broadcasted_iota(jnp.int32, (SLOTS, CH), 0)
    source = jnp.where(here - 1 < live, a * ROWS + here - 1, down * ROWS)
    source = jnp.where(here == 0, above_slot, source)
    one_hot = jnp.where(slot_row == source, 1.0, 0.0)
    chosen = jnp.dot(kpad[...], one_hot, precision=lax.Precision.HIGHEST, preferred_element_type=F32)
    for row in range(ROWS + 2):
        kbc[row] = jnp.broadcast_to(chosen[:, row : row + 1], (16 * TAPS, CH))

    own1.wait()
    for half in range(2):
        for k in far_first:
            swap(send1, recv1, s1, r1, half, k).wait()
    load_tf.wait()
    spectra = jnp.dot(
        tfv[...], recv1[...].reshape(LON_DEV * LONP, CH), preferred_element_type=F32
    )
    lat_s1[...] = spectra.astype(BF16).reshape(LAT_DEV, 4, CH)

    x_own, y_own, z_own = lax.rem(a, X_DEV), lax.rem(a // X_DEV, Y_DEV), a // (X_DEV * Y_DEV)
    x_of = [lax.rem(x_own + dx, X_DEV) for dx in range(X_DEV)]
    z_base = [lax.rem(z_own + dz, Z_DEV) * (X_DEV * Y_DEV) for dz in range(Z_DEV)]
    across = [(dz, dx) for dz in (1, 2, 0) for dx in (2, 1, 3, 0)]

    def all_lat(sent, got, which):
        own = pltpu.make_async_copy(sent.at[a], got.at[a], lr.at[which])
        own.start()

        def send(along_y, across):
            y = lax.rem(y_own + along_y, Y_DEV) * X_DEV
            for dz, dx in across:
                j = z_base[dz] + y + x_of[dx]
                pltpu.make_async_remote_copy(
                    src_ref=sent.at[j], dst_ref=got.at[a], send_sem=ls.at[which],
                    recv_sem=lr.at[which], device_id=(j, d), device_id_type=MESH,
                ).start()

        def farther(i, carry):
            off = (i + 1) // 2
            send(jnp.where(lax.rem(i, 2) == 1, Y_DEV // 2 - off, Y_DEV // 2 + off), across)
            return carry

        lax.fori_loop(0, Y_DEV - 1, farther, 0)
        send(0, across[:-1])
        pltpu.make_async_copy(sent, got, lr.at[which]).wait()

    all_lat(lat_s1, lat_r1, 0)

    coltmp[...] = lat_r1[...].astype(F32).reshape(COEF, CH)
    block_slot = lax.broadcasted_iota(jnp.int32, (LAT_DEV, ROWS, CH), 1)
    block_group = lax.broadcasted_iota(jnp.int32, (LAT_DEV, ROWS, CH), 2) // SHARE
    diagonal = block_slot == block_group
    for q in range(4):
        column = coltmp[pl.ds(q, LAT_DEV, stride=4), :]
        wide = jnp.where(diagonal, column[:, None, :], 0.0)
        rhs[:, pl.ds(q * CH, CH)] = wide.reshape(SLOTS, CH).astype(BF16)
    for mm in range(2):
        coef = jnp.dot(legb[mm], rhs[:, pl.ds(mm * 2 * CH, 2 * CH)], preferred_element_type=F32)
        parts = []
        for part in range(2):
            folded = coef[:, part * CH : (part + 1) * CH]
            for step in (SHARE, 2 * SHARE, 4 * SHARE):
                folded = folded + pltpu.roll(folded, step, 1)
            parts.append(folded)
        real, imag = parts
        fr, fi = filtr[0], filtr[1]
        filtered = jnp.concatenate([fr * real + fi * imag, fr * imag - fi * real], axis=1)
        back = jnp.dot(legt[mm], filtered.astype(BF16), preferred_element_type=F32)
        for part in range(2):
            wide = back[:, part * CH : (part + 1) * CH].reshape(LAT_DEV, ROWS, CH)
            wide = jnp.where(diagonal, wide, 0.0).astype(BF16)
            zed[:, pl.ds((2 * mm + part) * CH, CH)] = wide.reshape(SLOTS, CH)
    returned = jnp.dot(pick[...], zed[...], preferred_element_type=F32)
    for q in range(4):
        coltmp[pl.ds(q, LAT_DEV, stride=4), :] = returned[:, q * CH : (q + 1) * CH]
    lat_s2[...] = coltmp[...].astype(BF16).reshape(LAT_DEV, 4, CH)
    all_lat(lat_s2, lat_r2, 1)

    load_ti.wait()
    modes = lat_r2[...].reshape(COEF, CH)

    def block_of(p, half):
        part = pl.ds(half * HALF, HALF)
        send2[p, part, :] = jnp.dot(tiv[p, part, :], modes, preferred_element_type=F32).astype(BF16)

    for half in range(2):
        for k in far_first:
            block_of(partner(k), half)
            swap(send2, recv2, s2, r2, half, k).start()
    for half in range(2):
        block_of(d, half)
    own2 = pltpu.make_async_copy(send2.at[d], recv2.at[d], own_sem.at[1])
    own2.start()

    load_w.wait()
    wf[...] = wv[...].astype(F32)

    def weights(step, carry):
        row, half = step // 2, lax.rem(step, 2)
        o = pl.multiple_of(half * 64, 64)
        for t in range(TAPS):
            total = None
            for k in range(KINDS):
                part = wf[k, pl.ds(o, 64), :] * kbc[row, pl.ds(16 * t + k, 1), :]
                total = part if total is None else total + part
            tap_row, tap_col = t // 3, t % 3
            weff[row, pl.ds(tap_col * CH + o, 64), pl.ds(tap_row * CH, CH)] = total.astype(BF16)
        return carry

    lax.fori_loop(0, 2 * (ROWS + 2), weights, 0)

    for copy in edges:
        copy.wait()
    has_above = a > 0
    has_below = a < LAT_DEV - 1
    above_row = jnp.where(has_above, row_r[0].astype(F32), 0.0)
    below_row = jnp.where(has_below, row_r[1].astype(F32), 0.0)
    ext[0, pl.ds(EDGE, LONP), :] = above_row
    for slot in range(1, ROWS):
        old = ext[slot + 1, pl.ds(EDGE, LONP), :]
        ext[slot + 1, pl.ds(EDGE, LONP), :] = jnp.where(live == slot, below_row, old)
    ext[ROWS + 1, pl.ds(EDGE, LONP), :] = jnp.where(live == ROWS, below_row, 0.0)
    for side, at in ((0, EDGE - 1), (1, EDGE + LON)):
        slots = cell_r[side].astype(F32)
        above_cell = jnp.where(has_above, cell_r[2 + side].astype(F32), 0.0)
        below_cell = jnp.where(has_below, cell_r[4 + side].astype(F32), 0.0)
        ext[0, pl.ds(at, 1), :] = above_cell[0:1]
        for slot in range(ROWS + 1):
            edge_cell = jnp.where(live == slot, below_cell[0:1], slots[slot : slot + 1])
            ext[slot + 1, pl.ds(at, 1), :] = edge_cell

    for spare in (0, 1, ROWS + 2, ROWS + 3):
        dsum[spare] = jnp.zeros((LONP, CH), F32)

    def stencil(row, carry):
        field = jnp.concatenate(
            [ext[row, pl.ds(EDGE - b, LONP), :] for b in (-1, 0, 1)], axis=1
        ).astype(BF16)
        taps = jnp.dot(field, weff[row], preferred_element_type=F32)
        for step in (-1, 0, 1):
            index = (step + 1) * CH
            dsum[row + step + 1] += taps[:, index : index + CH]
        return carry

    lax.fori_loop(0, ROWS + 2, stencil, 0)

    own2.wait()
    for half in range(2):
        for k in far_first:
            swap(send2, recv2, s2, r2, half, k).wait()
        for chunk in range(HALF // 16):
            first = half * HALF + chunk * 16
            blocks = [recv2[e, pl.ds(first, 16), :].astype(F32) for e in range(LON_DEV)]
            rows = exchange_groups(blocks, group16)
            for r in range(ROWS):
                total = dsum[r + 2, pl.ds(first, 16), :]
                total = total + rows[r] * qw_ref[a * ROWS + r]
                total = jnp.where(r < live, total, 0.0)
                outf[pl.ds(first * ROWS + r, 16, stride=ROWS), :] = total
        count = HALF if half == 0 else LON - HALF
        done = outf[pl.ds(half * HALF * ROWS, count * ROWS), :].astype(BF16)
        out_ref[pl.ds(half * HALF, count)] = done.reshape(count, ROWS, CH)

    for which, sent in ((0, lat_s1), (1, lat_s2)):
        most = sent.at[pl.ds(0, LAT_DEV - 1)]
        pltpu.make_async_copy(most, most, ls.at[which]).wait()


def on_device(grad_output, band_rows, legendre, quad_weights, spectral_filter, disco_kernel, disco_weight):
    forward, inverse = trig_tables()
    any_space = pl.BlockSpec(memory_space=pl.ANY)
    vmem = pltpu.VMEM
    dma = pltpu.SemaphoreType.DMA
    out = pl.pallas_call(
        kernel,
        out_shape=jax.ShapeDtypeStruct((LON, ROWS, CH), BF16),
        in_specs=[pl.BlockSpec(memory_space=pltpu.SMEM)] * 2 + [any_space] * 7,
        out_specs=pl.BlockSpec(memory_space=pltpu.VMEM),
        scratch_shapes=[
            vmem((LON, ROWS, CH), BF16),
            vmem((LONP * ROWS, CH), F32),
            vmem((ROWS + 2, LONP + 2 * EDGE, CH), F32),
            vmem((LON_DEV, LONP, CH), BF16),
            vmem((LON_DEV, LONP, CH), BF16),
            vmem((LAT_DEV, 4, CH), BF16),
            vmem((LAT_DEV, 4, CH), BF16),
            vmem((LAT_DEV, 4, CH), BF16),
            vmem((LAT_DEV, 4, CH), BF16),
            vmem((LON_DEV, LONP, CH), BF16),
            vmem((LON_DEV, LONP, CH), BF16),
            vmem((2, LONP, CH), BF16),
            vmem((2, LONP, CH), BF16),
            vmem((6, 16, CH), BF16),
            vmem((6, 16, CH), BF16),
            vmem((2, DEG, SLOTS), F32),
            vmem((2, DEGP, SLOTS), BF16),
            vmem((2, SLOTS, DEGP), BF16),
            vmem((2, DEG, CH), F32),
            vmem((2, DEGP, CH), F32),
            vmem((TAPS, KINDS, SLOTS), F32),
            vmem((16 * TAPS, SLOTS), F32),
            vmem((ROWS + 2, 16 * TAPS, CH), F32),
            vmem((KINDS, CH, CH), BF16),
            vmem((KINDS, CH, CH), F32),
            vmem((ROWS + 2, 3 * CH, 3 * CH), BF16),
            vmem((COEF, LON_DEV * LONP), BF16),
            vmem((LON_DEV, LONP, COEF), BF16),
            vmem((ROWS + 4, LONP, CH), F32),
            vmem((COEF, CH), F32),
            vmem((SLOTS, 4 * CH), BF16),
            vmem((SLOTS, 4 * CH), BF16),
            vmem((LAT_DEV, SLOTS), BF16),
            vmem((LONP * ROWS, CH), F32),
            dma((8,)),
            dma((2,)),
            dma((2, 8)),
            dma((2, 8)),
            dma((2, 8)),
            dma((2, 8)),
            dma((8,)),
            dma((8,)),
            dma((2,)),
            dma((2,)),
        ],
        compiler_params=pltpu.CompilerParams(
            collective_id=0, has_side_effects=True, vmem_limit_bytes=56 * 2**20
        ),
    )(
        band_rows,
        quad_weights,
        jnp.transpose(grad_output, (1, 0, 2)),
        legendre,
        spectral_filter,
        jnp.transpose(disco_kernel, (1, 2, 0)),
        jnp.transpose(disco_weight, (1, 0, 2)),
        jnp.asarray(forward),
        jnp.asarray(inverse),
    )
    return jnp.transpose(out, (1, 0, 2))


def solution(mesh):
    placed = (P("lat", "lon", None), P(), P("lat", None, None), P(), P(), P(), P())
    return jax.shard_map(
        on_device, mesh=mesh, in_specs=placed, out_specs=P("lat", "lon", None), check_vma=False
    )
```

```python
import jax
import jax.numpy as jnp
import ml_dtypes
import numpy as np
from jax import lax
from jax.experimental import pallas as pl
from jax.experimental.pallas import tpu as pltpu
from jax.sharding import PartitionSpec as P

MESH = pl.DeviceIdType.MESH
BF16 = jnp.bfloat16
F32 = jnp.float32

ROWS = 8
LON = 180
LONP = 192
HALF = LONP // 2
CH = 128
LON_DEV = 8
LAT_DEV = 96
X_DEV, Y_DEV, Z_DEV = 4, 8, 3
SHARE = CH // LON_DEV
MODES = 192
COEF = 2 * MODES
DEG = 360
DEGP = 384
SLOTS = LAT_DEV * ROWS
TAPS = 9
KINDS = 9
EDGE = 8


def trig_tables():
    points = LON * LON_DEV
    position = np.arange(points)[:, None]
    wavenumber = np.arange(MODES)[None, :]
    angle = (wavenumber * position % points) * (2.0 * np.pi / points)
    table = np.stack([np.cos(angle), -np.sin(angle)], axis=2) * points**-0.5
    blocks = np.zeros((LON_DEV, LONP, COEF))
    blocks[:, :LON] = table.reshape(LON_DEV, LON, COEF)
    parts = blocks.astype(ml_dtypes.bfloat16).reshape(LON_DEV, 2, HALF, LAT_DEV, 2, 2)
    forward = parts.transpose(1, 4, 3, 5, 0, 2).reshape(2, COEF, LON_DEV * HALF)
    inverse = parts.transpose(0, 1, 4, 2, 3, 5).reshape(LON_DEV, 4 * HALF, MODES)
    return np.ascontiguousarray(forward), np.ascontiguousarray(inverse)


def exchange_groups(rows, group_bit):
    rows = list(rows)
    for half in (4, 2, 1):
        low = (group_bit & half) == 0
        for r in range(ROWS):
            if r & half:
                continue
            a, b = rows[r], rows[r + half]
            rows[r] = jnp.where(low, a, pltpu.roll(b, SHARE * half, 1))
            rows[r + half] = jnp.where(low, pltpu.roll(a, CH - SHARE * half, 1), b)
    return rows


def kernel(
    rows_ref, qw_ref, g_ref, leg_ref, filt_ref, kern_ref, w_ref, tf_ref, ti_ref, out_ref,
    gv, xf, ext, send1, recv1, lat_s1, lat_r1, lat_s2, lat_r2, send2, recv2,
    row_s, row_r, cell_s, cell_r,
    legv, legb, legt, filtv, filtr, kernv, kpad, kbc, wv, wf, weff,
    tfv, tiv, dsum, coltmp, rhs, zed, pick, outf,
    load_sem, own_sem, s1, r1, s2, r2, hs, hr, ls, lr,
):
    a = lax.axis_index("lat")
    d = lax.axis_index("lon")
    up, down = lax.rem(a + LAT_DEV - 1, LAT_DEV), lax.rem(a + 1, LAT_DEV)
    west, east = lax.rem(d + LON_DEV - 1, LON_DEV), lax.rem(d + 1, LON_DEV)

    def load(i, src, dst):
        copy = pltpu.make_async_copy(src, dst, load_sem.at[i])
        copy.start()
        return copy

    load_g = (
        load(0, g_ref.at[pl.ds(0, HALF)], gv.at[pl.ds(0, HALF)]),
        load(7, g_ref.at[pl.ds(HALF, LON - HALF)], gv.at[pl.ds(HALF, LON - HALF)]),
    )

    barrier = pltpu.get_barrier_semaphore()

    def lat_after(k):
        j = a + k
        return jnp.where(j >= LAT_DEV, j - LAT_DEV, j)

    def greet(k, carry):
        pl.semaphore_signal(barrier, inc=1, device_id=(lat_after(k), d), device_id_type=MESH)
        return carry

    lax.fori_loop(1, LAT_DEV, greet, 0, unroll=5)
    for k in range(1, LON_DEV):
        pl.semaphore_signal(
            barrier, inc=1, device_id=(a, lax.rem(d + k, LON_DEV)), device_id_type=MESH
        )
    for lat in (up, down):
        for lon in (west, east):
            pl.semaphore_signal(barrier, inc=1, device_id=(lat, lon), device_id_type=MESH)
    load_leg = load(1, leg_ref, legv)
    load_filt = load(2, filt_ref, filtv)
    load_kern = load(3, kern_ref, kernv)
    load_w = load(4, w_ref, wv)
    load_tf = load(5, tf_ref, tfv)
    load_ti = load(6, ti_ref, tiv)

    live = rows_ref[a]
    group16 = lax.broadcasted_iota(jnp.int32, (16, CH), 1) // SHARE

    def partner(k):
        z, core = d // 2, lax.rem(d, 2)
        return lax.rem(z + k // 2, 4) * 2 + lax.rem(core + k % 2, 2)

    far_first = (4, 5, 2, 6, 3, 7, 1)

    def low_half(count):
        return (lax.broadcasted_iota(jnp.int32, (count, CH), 1) & 8) == 0

    low16 = low_half(16)

    def swap(sent, got, send_sem, recv_sem, half, k):
        p = partner(k)
        return pltpu.make_async_remote_copy(
            src_ref=sent.at[half, p], dst_ref=got.at[half, d], send_sem=send_sem.at[half, k],
            recv_sem=recv_sem.at[half, k], device_id=(a, p), device_id_type=MESH,
        )

    for half in range(2):
        load_g[half].wait()
        count = HALF if half == 0 else LON - HALF
        slot3 = lax.broadcasted_iota(jnp.int32, (count, ROWS, CH), 1)
        masked = jnp.where(slot3 < live, gv[pl.ds(half * HALF, count)].astype(F32), 0.0)
        xf[pl.ds(half * HALF * ROWS, count * ROWS), :] = masked.reshape(count * ROWS, CH)
        if half == 1:
            xf[pl.ds(LON * ROWS, (LONP - LON) * ROWS), :] = jnp.zeros(((LONP - LON) * ROWS, CH), F32)

    for chunk in range(HALF // 16):
        first = chunk * 16
        both = []
        for start in (first, first + HALF):
            rows = [xf[pl.ds(start * ROWS + r, 16, stride=ROWS), :] for r in range(ROWS)]
            both.append(exchange_groups(rows, group16))
        for p in range(LON_DEV):
            one, two = both[0][p], both[1][p]
            send1[0, p, pl.ds(first, 16), :] = jnp.where(low16, one, pltpu.roll(two, 8, 1)).astype(BF16)
            send1[1, p, pl.ds(first, 16), :] = jnp.where(low16, pltpu.roll(one, CH - 8, 1), two).astype(BF16)
    pl.semaphore_wait(barrier, LAT_DEV - 1 + LON_DEV - 1 + 4)
    for half in range(2):
        for k in far_first:
            swap(send1, recv1, s1, r1, half, k).start()
    own1 = [
        pltpu.make_async_copy(send1.at[half, d], recv1.at[half, d], own_sem.at[half])
        for half in range(2)
    ]
    for copy in own1:
        copy.start()

    for r in range(ROWS):
        row = xf[pl.ds(r, LONP, stride=ROWS), :]
        ext[r + 1, pl.ds(EDGE, LONP), :] = row
        dsum[r + 2] = row
        if r == 0:
            row_s[1] = row.astype(BF16)
            last_row = row
        else:
            last_row = jnp.where(live == r + 1, row, last_row)
    row_s[0] = last_row.astype(BF16)
    first_col = xf[pl.ds(0, ROWS), :]
    last_col = xf[pl.ds((LON - 1) * ROWS, ROWS), :]
    slot8 = lax.broadcasted_iota(jnp.int32, (ROWS, CH), 0)
    pad8 = jnp.zeros((ROWS, CH), F32)

    def cell_of(column, slot):
        cell = jnp.sum(jnp.where(slot8 == slot, column, 0.0), axis=0, keepdims=True)
        return jnp.broadcast_to(cell, (16, CH))

    cell_s[0] = jnp.concatenate([last_col, pad8], axis=0).astype(BF16)
    cell_s[1] = jnp.concatenate([first_col, pad8], axis=0).astype(BF16)
    cell_s[2] = cell_of(last_col, live - 1).astype(BF16)
    cell_s[3] = cell_of(first_col, live - 1).astype(BF16)
    cell_s[4] = cell_of(last_col, 0).astype(BF16)
    cell_s[5] = cell_of(first_col, 0).astype(BF16)
    targets = ((a, east), (a, west), (down, east), (down, west), (up, east), (up, west))
    edges = [
        pltpu.make_async_remote_copy(
            src_ref=cell_s.at[i], dst_ref=cell_r.at[i], send_sem=hs.at[i], recv_sem=hr.at[i],
            device_id=target, device_id_type=MESH,
        )
        for i, target in enumerate(targets)
    ] + [
        pltpu.make_async_remote_copy(
            src_ref=row_s.at[i], dst_ref=row_r.at[i], send_sem=hs.at[6 + i], recv_sem=hr.at[6 + i],
            device_id=(lat, d), device_id_type=MESH,
        )
        for i, lat in enumerate((down, up))
    ]
    for copy in edges:
        copy.start()

    load_leg.wait()
    legb[...] = jnp.zeros_like(legb)
    for mm in range(2):
        legb[mm, pl.ds(0, DEG), :] = legv[mm].astype(BF16)
    zero_rows = jnp.zeros((DEGP - DEG, CH), F32)

    for mm in range(2):
        for block in range(SLOTS // CH):
            at = block * CH
            tile = jnp.concatenate([legv[mm, :, pl.ds(at, CH)], zero_rows], axis=0)
            legt[mm, pl.ds(at, CH), :] = tile.T.astype(BF16)

    load_filt.wait()
    lane = lax.broadcasted_iota(jnp.int32, (DEG, CH), 1)
    filtr[...] = jnp.zeros_like(filtr)
    for part in range(2):
        for half in range(2):
            mine = pltpu.roll(filtv[part], lax.rem(2 * CH - SHARE * d - 8 * half, CH), 1)
            mine = jnp.where(lane < 8, mine, 0.0)
            for step in (8, 16, 32, 64):
                mine = mine + pltpu.roll(mine, step, 1)
            filtr[half, part, pl.ds(0, DEG), :] = mine

    band_row = lax.broadcasted_iota(jnp.int32, (LAT_DEV, SLOTS), 0)
    band_col = lax.broadcasted_iota(jnp.int32, (LAT_DEV, SLOTS), 1) // ROWS
    pick[...] = jnp.where(band_row == band_col, 1.0, 0.0).astype(BF16)

    load_kern.wait()
    kpad[...] = jnp.zeros_like(kpad)
    for t in range(TAPS):
        kpad[pl.ds(16 * t, KINDS), :] = kernv[t]
    above_slot = up * ROWS + rows_ref[up] - 1
    here = lax.broadcasted_iota(jnp.int32, (SLOTS, CH), 1)
    slot_row = lax.broadcasted_iota(jnp.int32, (SLOTS, CH), 0)
    source = jnp.where(here - 1 < live, a * ROWS + here - 1, down * ROWS)
    source = jnp.where(here == 0, above_slot, source)
    one_hot = jnp.where(slot_row == source, 1.0, 0.0)
    chosen = jnp.dot(kpad[...], one_hot, precision=lax.Precision.HIGHEST, preferred_element_type=F32)
    for row in range(ROWS + 2):
        kbc[row] = jnp.broadcast_to(chosen[:, row : row + 1], (16 * TAPS, CH))

    load_tf.wait()
    x_own, y_own, z_own = lax.rem(a, X_DEV), lax.rem(a // X_DEV, Y_DEV), a // (X_DEV * Y_DEV)
    x_of = [lax.rem(x_own + dx, X_DEV) for dx in range(X_DEV)]
    z_base = [lax.rem(z_own + dz, Z_DEV) * (X_DEV * Y_DEV) for dz in range(Z_DEV)]
    across = [(dz, dx) for dz in (1, 2, 0) for dx in (2, 1, 3, 0)]

    def all_lat(sent, got, which):
        own = pltpu.make_async_copy(sent.at[a], got.at[a], lr.at[which])
        own.start()

        def send(along_y, across):
            y = lax.rem(y_own + along_y, Y_DEV) * X_DEV
            for dz, dx in across:
                j = z_base[dz] + y + x_of[dx]
                pltpu.make_async_remote_copy(
                    src_ref=sent.at[j], dst_ref=got.at[a], send_sem=ls.at[which],
                    recv_sem=lr.at[which], device_id=(j, d), device_id_type=MESH,
                ).start()

        def farther(i, carry):
            off = (i + 1) // 2
            send(jnp.where(lax.rem(i, 2) == 1, Y_DEV // 2 - off, Y_DEV // 2 + off), across)
            return carry

        lax.fori_loop(0, Y_DEV - 1, farther, 0)
        send(0, across[:-1])

    low_rows = low_half(MODES)
    for half in range(2):
        own1[half].wait()
        for k in far_first:
            swap(send1, recv1, s1, r1, half, k).wait()
        field = recv1[half].reshape(LON_DEV * HALF, CH)
        one = jnp.dot(tfv[0], field, preferred_element_type=F32)
        two = jnp.dot(tfv[1], field, preferred_element_type=F32)
        even = one[:MODES] + pltpu.roll(two[:MODES], CH - 8, 1)
        odd = pltpu.roll(one[MODES:], 8, 1) + two[MODES:]
        spectra = jnp.where(low_rows, even, odd).astype(BF16)
        lat_s1[half] = spectra.reshape(LAT_DEV, 2, CH)
        all_lat(lat_s1.at[half], lat_r1.at[half], half)

    block_slot = lax.broadcasted_iota(jnp.int32, (LAT_DEV, ROWS, CH), 1)
    block_lane = lax.broadcasted_iota(jnp.int32, (LAT_DEV, ROWS, CH), 2)
    diagonal = block_slot == block_lane // SHARE
    low_slots = (lax.broadcasted_iota(jnp.int32, (SLOTS, 2 * CH), 1) & 8) == 0
    low_degrees = (lax.broadcasted_iota(jnp.int32, (DEGP, 2 * CH), 1) & 8) == 0
    for half in range(2):
        pltpu.make_async_copy(lat_s1.at[half], lat_r1.at[half], lr.at[half]).wait()
        coltmp[half] = lat_r1[half].astype(F32).reshape(2 * LAT_DEV, CH)
        for q in range(2):
            column = coltmp[half, pl.ds(q, LAT_DEV, stride=2), :]
            wide = jnp.where(diagonal, column[:, None, :], 0.0)
            rhs[half, :, pl.ds(q * CH, CH)] = wide.reshape(SLOTS, CH).astype(BF16)
        coef = jnp.where(
            low_degrees,
            jnp.dot(legb[0], rhs[half], preferred_element_type=F32),
            jnp.dot(legb[1], rhs[half], preferred_element_type=F32),
        )
        parts = []
        for part in range(2):
            folded = coef[:, part * CH : (part + 1) * CH]
            for step in (SHARE, 2 * SHARE, 4 * SHARE):
                folded = folded + pltpu.roll(folded, step, 1)
            parts.append(folded)
        real, imag = parts
        fr, fi = filtr[half, 0], filtr[half, 1]
        filtered = jnp.concatenate([fr * real + fi * imag, fr * imag - fi * real], axis=1).astype(BF16)
        back = jnp.where(
            low_slots,
            jnp.dot(legt[0], filtered, preferred_element_type=F32),
            jnp.dot(legt[1], filtered, preferred_element_type=F32),
        )
        for part in range(2):
            wide = back[:, part * CH : (part + 1) * CH].reshape(LAT_DEV, ROWS, CH)
            wide = jnp.where(diagonal, wide, 0.0).astype(BF16)
            zed[half, :, pl.ds(part * CH, CH)] = wide.reshape(SLOTS, CH)
        returned = jnp.dot(pick[...], zed[half], preferred_element_type=F32)
        for q in range(2):
            coltmp[half, pl.ds(q, LAT_DEV, stride=2), :] = returned[:, q * CH : (q + 1) * CH]
        lat_s2[half] = coltmp[half].astype(BF16).reshape(LAT_DEV, 2, CH)
        all_lat(lat_s2.at[half], lat_r2.at[half], 2 + half)

    load_ti.wait()
    low_block = low_half(HALF)

    def block_of(p, half, modes):
        four = jnp.dot(tiv[p], modes, preferred_element_type=F32)
        first = four[:HALF] + pltpu.roll(four[HALF : 2 * HALF], CH - 8, 1)
        second = pltpu.roll(four[2 * HALF : 3 * HALF], 8, 1) + four[3 * HALF :]
        send2[half, p] = jnp.where(low_block, first, second).astype(BF16)

    own2 = []
    for half in range(2):
        pltpu.make_async_copy(lat_s2.at[half], lat_r2.at[half], lr.at[2 + half]).wait()
        modes = lat_r2[half].reshape(MODES, CH)
        for k in far_first:
            block_of(partner(k), half, modes)
            swap(send2, recv2, s2, r2, half, k).start()
        block_of(d, half, modes)
        own2.append(
            pltpu.make_async_copy(send2.at[half, d], recv2.at[half, d], own_sem.at[2 + half])
        )
        own2[half].start()

    load_w.wait()
    wf[...] = wv[...].astype(F32)

    def weights(step, carry):
        row, half = step // 2, lax.rem(step, 2)
        o = pl.multiple_of(half * 64, 64)
        for t in range(TAPS):
            total = None
            for k in range(KINDS):
                part = wf[k, pl.ds(o, 64), :] * kbc[row, pl.ds(16 * t + k, 1), :]
                total = part if total is None else total + part
            tap_row, tap_col = t // 3, t % 3
            weff[row, pl.ds(tap_col * CH + o, 64), pl.ds(tap_row * CH, CH)] = total.astype(BF16)
        return carry

    lax.fori_loop(0, 2 * (ROWS + 2), weights, 0)

    for copy in edges:
        copy.wait()
    has_above = a > 0
    has_below = a < LAT_DEV - 1
    above_row = jnp.where(has_above, row_r[0].astype(F32), 0.0)
    below_row = jnp.where(has_below, row_r[1].astype(F32), 0.0)
    ext[0, pl.ds(EDGE, LONP), :] = above_row
    for slot in range(1, ROWS):
        old = ext[slot + 1, pl.ds(EDGE, LONP), :]
        ext[slot + 1, pl.ds(EDGE, LONP), :] = jnp.where(live == slot, below_row, old)
    ext[ROWS + 1, pl.ds(EDGE, LONP), :] = jnp.where(live == ROWS, below_row, 0.0)
    for side, at in ((0, EDGE - 1), (1, EDGE + LON)):
        slots = cell_r[side].astype(F32)
        above_cell = jnp.where(has_above, cell_r[2 + side].astype(F32), 0.0)
        below_cell = jnp.where(has_below, cell_r[4 + side].astype(F32), 0.0)
        ext[0, pl.ds(at, 1), :] = above_cell[0:1]
        for slot in range(ROWS + 1):
            edge_cell = jnp.where(live == slot, below_cell[0:1], slots[slot : slot + 1])
            ext[slot + 1, pl.ds(at, 1), :] = edge_cell

    for spare in (0, 1, ROWS + 2, ROWS + 3):
        dsum[spare] = jnp.zeros((LONP, CH), F32)

    def stencil(row, carry):
        field = jnp.concatenate(
            [ext[row, pl.ds(EDGE - b, LONP), :] for b in (-1, 0, 1)], axis=1
        ).astype(BF16)
        taps = jnp.dot(field, weff[row], preferred_element_type=F32)
        for step in (-1, 0, 1):
            index = (step + 1) * CH
            dsum[row + step + 1] += taps[:, index : index + CH]
        return carry

    lax.fori_loop(0, ROWS + 2, stencil, 0)

    for half in range(2):
        own2[half].wait()
        for k in far_first:
            swap(send2, recv2, s2, r2, half, k).wait()
    for chunk in range(HALF // 16):
        begin = chunk * 16
        blocks = ([], [])
        for e in range(LON_DEV):
            one = recv2[0, e, pl.ds(begin, 16), :].astype(F32)
            two = recv2[1, e, pl.ds(begin, 16), :].astype(F32)
            blocks[0].append(jnp.where(low16, one, pltpu.roll(two, 8, 1)))
            blocks[1].append(jnp.where(low16, pltpu.roll(one, CH - 8, 1), two))
        for half in range(2):
            first = half * HALF + begin
            rows = exchange_groups(blocks[half], group16)
            for r in range(ROWS):
                total = dsum[r + 2, pl.ds(first, 16), :]
                total = total + rows[r] * qw_ref[a * ROWS + r]
                total = jnp.where(r < live, total, 0.0)
                outf[pl.ds(first * ROWS + r, 16, stride=ROWS), :] = total
    out_ref[...] = outf[pl.ds(0, LON * ROWS), :].astype(BF16).reshape(LON, ROWS, CH)

    for half in range(2):
        for which, sent in ((half, lat_s1), (2 + half, lat_s2)):
            most = sent.at[half, pl.ds(0, LAT_DEV - 1)]
            pltpu.make_async_copy(most, most, ls.at[which]).wait()


def on_device(grad_output, band_rows, legendre, quad_weights, spectral_filter, disco_kernel, disco_weight):
    forward, inverse = trig_tables()
    any_space = pl.BlockSpec(memory_space=pl.ANY)
    vmem = pltpu.VMEM
    dma = pltpu.SemaphoreType.DMA
    out = pl.pallas_call(
        kernel,
        out_shape=jax.ShapeDtypeStruct((LON, ROWS, CH), BF16),
        in_specs=[pl.BlockSpec(memory_space=pltpu.SMEM)] * 2 + [any_space] * 7,
        out_specs=pl.BlockSpec(memory_space=pltpu.VMEM),
        scratch_shapes=[
            vmem((LON, ROWS, CH), BF16),
            vmem((LONP * ROWS, CH), F32),
            vmem((ROWS + 2, LONP + 2 * EDGE, CH), F32),
            vmem((2, LON_DEV, HALF, CH), BF16),
            vmem((2, LON_DEV, HALF, CH), BF16),
            vmem((2, LAT_DEV, 2, CH), BF16),
            vmem((2, LAT_DEV, 2, CH), BF16),
            vmem((2, LAT_DEV, 2, CH), BF16),
            vmem((2, LAT_DEV, 2, CH), BF16),
            vmem((2, LON_DEV, HALF, CH), BF16),
            vmem((2, LON_DEV, HALF, CH), BF16),
            vmem((2, LONP, CH), BF16),
            vmem((2, LONP, CH), BF16),
            vmem((6, 16, CH), BF16),
            vmem((6, 16, CH), BF16),
            vmem((2, DEG, SLOTS), F32),
            vmem((2, DEGP, SLOTS), BF16),
            vmem((2, SLOTS, DEGP), BF16),
            vmem((2, DEG, CH), F32),
            vmem((2, 2, DEGP, CH), F32),
            vmem((TAPS, KINDS, SLOTS), F32),
            vmem((16 * TAPS, SLOTS), F32),
            vmem((ROWS + 2, 16 * TAPS, CH), F32),
            vmem((KINDS, CH, CH), BF16),
            vmem((KINDS, CH, CH), F32),
            vmem((ROWS + 2, 3 * CH, 3 * CH), BF16),
            vmem((2, COEF, LON_DEV * HALF), BF16),
            vmem((LON_DEV, 4 * HALF, MODES), BF16),
            vmem((ROWS + 4, LONP, CH), F32),
            vmem((2, 2 * LAT_DEV, CH), F32),
            vmem((2, SLOTS, 2 * CH), BF16),
            vmem((2, SLOTS, 2 * CH), BF16),
            vmem((LAT_DEV, SLOTS), BF16),
            vmem((LONP * ROWS, CH), F32),
            dma((8,)),
            dma((4,)),
            dma((2, 8)),
            dma((2, 8)),
            dma((2, 8)),
            dma((2, 8)),
            dma((8,)),
            dma((8,)),
            dma((4,)),
            dma((4,)),
        ],
        compiler_params=pltpu.CompilerParams(
            collective_id=0, has_side_effects=True, vmem_limit_bytes=56 * 2**20
        ),
    )(
        band_rows,
        quad_weights,
        jnp.transpose(grad_output, (1, 0, 2)),
        legendre,
        spectral_filter,
        jnp.transpose(disco_kernel, (1, 2, 0)),
        jnp.transpose(disco_weight, (1, 0, 2)),
        jnp.asarray(forward),
        jnp.asarray(inverse),
    )
    return jnp.transpose(out, (1, 0, 2))


def solution(mesh):
    placed = (P("lat", "lon", None), P(), P("lat", None, None), P(), P(), P(), P())
    return jax.shard_map(
        on_device, mesh=mesh, in_specs=placed, out_specs=P("lat", "lon", None), check_vma=False
    )
```

```python
import jax
import jax.numpy as jnp
import ml_dtypes
import numpy as np
from jax import lax
from jax.experimental import pallas as pl
from jax.experimental.pallas import tpu as pltpu
from jax.sharding import PartitionSpec as P

MESH = pl.DeviceIdType.MESH
BF16 = jnp.bfloat16
F32 = jnp.float32

ROWS = 8
LON = 180
LONP = 192
HALF = LONP // 2
CH = 128
LON_DEV = 8
LAT_DEV = 96
X_DEV, Y_DEV, Z_DEV = 4, 8, 3
SHARE = CH // LON_DEV
MODES = 192
COEF = 2 * MODES
DEG = 360
DEGP = 384
SLOTS = LAT_DEV * ROWS
TAPS = 9
KINDS = 9
EDGE = 8


def trig_tables():
    points = LON * LON_DEV
    position = np.arange(points)[:, None]
    wavenumber = np.arange(MODES)[None, :]
    angle = (wavenumber * position % points) * (2.0 * np.pi / points)
    table = np.stack([np.cos(angle), -np.sin(angle)], axis=2) * points**-0.5
    blocks = np.zeros((LON_DEV, LONP, COEF))
    blocks[:, :LON] = table.reshape(LON_DEV, LON, COEF)
    parts = blocks.astype(ml_dtypes.bfloat16).reshape(LON_DEV, 2, HALF, LAT_DEV, 2, 2)
    forward = parts.transpose(1, 4, 3, 5, 0, 2).reshape(2, COEF, LON_DEV * HALF)
    inverse = parts.transpose(0, 1, 4, 2, 3, 5).reshape(LON_DEV, 4 * HALF, MODES)
    return np.ascontiguousarray(forward), np.ascontiguousarray(inverse)


def exchange_groups(rows, group_bit):
    rows = list(rows)
    for half in (4, 2, 1):
        low = (group_bit & half) == 0
        for r in range(ROWS):
            if r & half:
                continue
            a, b = rows[r], rows[r + half]
            rows[r] = jnp.where(low, a, pltpu.roll(b, SHARE * half, 1))
            rows[r + half] = jnp.where(low, pltpu.roll(a, CH - SHARE * half, 1), b)
    return rows


def kernel(
    rows_ref, qw_ref, g_ref, leg_ref, filt_ref, kern_ref, w_ref, tf_ref, ti_ref, out_ref,
    gv, xf, ext, send1, recv1, lat_s1, lat_r1, lat_s2, lat_r2, send2, recv2,
    row_s, row_r, cell_s, cell_r,
    legv, legb, legt, filtv, filtr, kernv, kpad, kbc, wv, wf, weff,
    tfv, tiv, dsum, coltmp, rhs, zed, pick, outf,
    load_sem, own_sem, s1, r1, s2, r2, hs, hr, ls, lr,
):
    a = lax.axis_index("lat")
    d = lax.axis_index("lon")
    up, down = lax.rem(a + LAT_DEV - 1, LAT_DEV), lax.rem(a + 1, LAT_DEV)
    west, east = lax.rem(d + LON_DEV - 1, LON_DEV), lax.rem(d + 1, LON_DEV)

    def load(i, src, dst):
        copy = pltpu.make_async_copy(src, dst, load_sem.at[i])
        copy.start()
        return copy

    load_g = (
        load(0, g_ref.at[pl.ds(0, HALF)], gv.at[pl.ds(0, HALF)]),
        load(7, g_ref.at[pl.ds(HALF, LON - HALF)], gv.at[pl.ds(HALF, LON - HALF)]),
    )

    barrier = pltpu.get_barrier_semaphore()

    def lat_after(k):
        j = a + k
        return jnp.where(j >= LAT_DEV, j - LAT_DEV, j)

    def greet(k, carry):
        pl.semaphore_signal(barrier, inc=1, device_id=(lat_after(k), d), device_id_type=MESH)
        return carry

    lax.fori_loop(1, LAT_DEV, greet, 0, unroll=5)
    for k in range(1, LON_DEV):
        pl.semaphore_signal(
            barrier, inc=1, device_id=(a, lax.rem(d + k, LON_DEV)), device_id_type=MESH
        )
    for lat in (up, down):
        for lon in (west, east):
            pl.semaphore_signal(barrier, inc=1, device_id=(lat, lon), device_id_type=MESH)
    load_leg = load(1, leg_ref, legv)
    load_filt = load(2, filt_ref, filtv)
    load_kern = load(3, kern_ref, kernv)
    load_w = load(4, w_ref, wv)
    load_tf = load(5, tf_ref, tfv)
    load_ti = load(6, ti_ref, tiv)

    live = rows_ref[a]
    group16 = lax.broadcasted_iota(jnp.int32, (16, CH), 1) // SHARE

    def partner(k):
        z, core = d // 2, lax.rem(d, 2)
        return lax.rem(z + k // 2, 4) * 2 + lax.rem(core + k % 2, 2)

    far_first = (4, 5, 2, 6, 3, 7, 1)

    def low_half(count):
        return (lax.broadcasted_iota(jnp.int32, (count, CH), 1) & 8) == 0

    low16 = low_half(16)

    def swap(sent, got, send_sem, recv_sem, half, k):
        p = partner(k)
        return pltpu.make_async_remote_copy(
            src_ref=sent.at[half, p], dst_ref=got.at[half, d], send_sem=send_sem.at[half, k],
            recv_sem=recv_sem.at[half, k], device_id=(a, p), device_id_type=MESH,
        )

    for half in range(2):
        load_g[half].wait()
        count = HALF if half == 0 else LON - HALF
        slot3 = lax.broadcasted_iota(jnp.int32, (count, ROWS, CH), 1)
        masked = jnp.where(slot3 < live, gv[pl.ds(half * HALF, count)].astype(F32), 0.0)
        xf[pl.ds(half * HALF * ROWS, count * ROWS), :] = masked.reshape(count * ROWS, CH)
        if half == 1:
            xf[pl.ds(LON * ROWS, (LONP - LON) * ROWS), :] = jnp.zeros(((LONP - LON) * ROWS, CH), F32)

    for chunk in range(HALF // 16):
        first = chunk * 16
        both = []
        for start in (first, first + HALF):
            rows = [xf[pl.ds(start * ROWS + r, 16, stride=ROWS), :] for r in range(ROWS)]
            both.append(exchange_groups(rows, group16))
        for p in range(LON_DEV):
            one, two = both[0][p], both[1][p]
            send1[0, p, pl.ds(first, 16), :] = jnp.where(low16, one, pltpu.roll(two, 8, 1)).astype(BF16)
            send1[1, p, pl.ds(first, 16), :] = jnp.where(low16, pltpu.roll(one, CH - 8, 1), two).astype(BF16)
    pl.semaphore_wait(barrier, LAT_DEV - 1 + LON_DEV - 1 + 4)
    for half in range(2):
        for k in far_first:
            swap(send1, recv1, s1, r1, half, k).start()
    own1 = [
        pltpu.make_async_copy(send1.at[half, d], recv1.at[half, d], own_sem.at[half])
        for half in range(2)
    ]
    for copy in own1:
        copy.start()

    for r in range(ROWS):
        row = xf[pl.ds(r, LONP, stride=ROWS), :]
        ext[r + 1, pl.ds(EDGE, LONP), :] = row
        dsum[r + 2] = row
        if r == 0:
            row_s[1] = row.astype(BF16)
            last_row = row
        else:
            last_row = jnp.where(live == r + 1, row, last_row)
    row_s[0] = last_row.astype(BF16)
    first_col = xf[pl.ds(0, ROWS), :]
    last_col = xf[pl.ds((LON - 1) * ROWS, ROWS), :]
    slot8 = lax.broadcasted_iota(jnp.int32, (ROWS, CH), 0)
    pad8 = jnp.zeros((ROWS, CH), F32)

    def cell_of(column, slot):
        cell = jnp.sum(jnp.where(slot8 == slot, column, 0.0), axis=0, keepdims=True)
        return jnp.broadcast_to(cell, (16, CH))

    cell_s[0] = jnp.concatenate([last_col, pad8], axis=0).astype(BF16)
    cell_s[1] = jnp.concatenate([first_col, pad8], axis=0).astype(BF16)
    cell_s[2] = cell_of(last_col, live - 1).astype(BF16)
    cell_s[3] = cell_of(first_col, live - 1).astype(BF16)
    cell_s[4] = cell_of(last_col, 0).astype(BF16)
    cell_s[5] = cell_of(first_col, 0).astype(BF16)
    targets = ((a, east), (a, west), (down, east), (down, west), (up, east), (up, west))
    edges = [
        pltpu.make_async_remote_copy(
            src_ref=cell_s.at[i], dst_ref=cell_r.at[i], send_sem=hs.at[i], recv_sem=hr.at[i],
            device_id=target, device_id_type=MESH,
        )
        for i, target in enumerate(targets)
    ] + [
        pltpu.make_async_remote_copy(
            src_ref=row_s.at[i], dst_ref=row_r.at[i], send_sem=hs.at[6 + i], recv_sem=hr.at[6 + i],
            device_id=(lat, d), device_id_type=MESH,
        )
        for i, lat in enumerate((down, up))
    ]
    for copy in edges:
        copy.start()

    load_leg.wait()
    legb[...] = jnp.zeros_like(legb)
    for mm in range(2):
        legb[mm, pl.ds(0, DEG), :] = legv[mm].astype(BF16)
    zero_rows = jnp.zeros((DEGP - DEG, CH), F32)

    for mm in range(2):
        for block in range(SLOTS // CH):
            at = block * CH
            tile = jnp.concatenate([legv[mm, :, pl.ds(at, CH)], zero_rows], axis=0)
            legt[mm, pl.ds(at, CH), :] = tile.T.astype(BF16)

    load_filt.wait()
    lane = lax.broadcasted_iota(jnp.int32, (DEG, CH), 1)
    filtr[...] = jnp.zeros_like(filtr)
    for part in range(2):
        for half in range(2):
            mine = pltpu.roll(filtv[part], lax.rem(2 * CH - SHARE * d - 8 * half, CH), 1)
            mine = jnp.where(lane < 8, mine, 0.0)
            for step in (8, 16, 32, 64):
                mine = mine + pltpu.roll(mine, step, 1)
            filtr[half, part, pl.ds(0, DEG), :] = mine

    band_row = lax.broadcasted_iota(jnp.int32, (LAT_DEV, SLOTS), 0)
    band_col = lax.broadcasted_iota(jnp.int32, (LAT_DEV, SLOTS), 1) // ROWS
    pick[...] = jnp.where(band_row == band_col, 1.0, 0.0).astype(BF16)

    load_tf.wait()
    x_own, y_own, z_own = lax.rem(a, X_DEV), lax.rem(a // X_DEV, Y_DEV), a // (X_DEV * Y_DEV)
    x_of = [lax.rem(x_own + dx, X_DEV) for dx in range(X_DEV)]
    z_base = [lax.rem(z_own + dz, Z_DEV) * (X_DEV * Y_DEV) for dz in range(Z_DEV)]
    across = [(dz, dx) for dz in (1, 2, 0) for dx in (2, 1, 3, 0)]

    def all_lat(sent, got, which):
        own = pltpu.make_async_copy(sent.at[a], got.at[a], lr.at[which])
        own.start()

        def send(along_y, across):
            y = lax.rem(y_own + along_y, Y_DEV) * X_DEV
            for dz, dx in across:
                j = z_base[dz] + y + x_of[dx]
                pltpu.make_async_remote_copy(
                    src_ref=sent.at[j], dst_ref=got.at[a], send_sem=ls.at[which],
                    recv_sem=lr.at[which], device_id=(j, d), device_id_type=MESH,
                ).start()

        def farther(i, carry):
            off = (i + 1) // 2
            send(jnp.where(lax.rem(i, 2) == 1, Y_DEV // 2 - off, Y_DEV // 2 + off), across)
            return carry

        lax.fori_loop(0, Y_DEV - 1, farther, 0)
        send(0, across[:-1])

    low_rows = low_half(MODES)
    for half in range(2):
        own1[half].wait()
        for k in far_first:
            swap(send1, recv1, s1, r1, half, k).wait()
        field = recv1[half].reshape(LON_DEV * HALF, CH)
        one = jnp.dot(tfv[0], field, preferred_element_type=F32)
        two = jnp.dot(tfv[1], field, preferred_element_type=F32)
        even = one[:MODES] + pltpu.roll(two[:MODES], CH - 8, 1)
        odd = pltpu.roll(one[MODES:], 8, 1) + two[MODES:]
        spectra = jnp.where(low_rows, even, odd).astype(BF16)
        lat_s1[half] = spectra.reshape(LAT_DEV, 2, CH)
        all_lat(lat_s1.at[half], lat_r1.at[half], half)

    block_slot = lax.broadcasted_iota(jnp.int32, (LAT_DEV, ROWS, CH), 1)
    block_lane = lax.broadcasted_iota(jnp.int32, (LAT_DEV, ROWS, CH), 2)
    diagonal = block_slot == block_lane // SHARE
    low_slots = (lax.broadcasted_iota(jnp.int32, (SLOTS, 2 * CH), 1) & 8) == 0
    low_degrees = (lax.broadcasted_iota(jnp.int32, (DEGP, 2 * CH), 1) & 8) == 0
    for half in range(2):
        pltpu.make_async_copy(lat_s1.at[half], lat_r1.at[half], lr.at[half]).wait()
        coltmp[half] = lat_r1[half].astype(F32).reshape(2 * LAT_DEV, CH)
        for q in range(2):
            column = coltmp[half, pl.ds(q, LAT_DEV, stride=2), :]
            wide = jnp.where(diagonal, column[:, None, :], 0.0)
            rhs[half, :, pl.ds(q * CH, CH)] = wide.reshape(SLOTS, CH).astype(BF16)
        coef = jnp.where(
            low_degrees,
            jnp.dot(legb[0], rhs[half], preferred_element_type=F32),
            jnp.dot(legb[1], rhs[half], preferred_element_type=F32),
        )
        parts = []
        for part in range(2):
            folded = coef[:, part * CH : (part + 1) * CH]
            for step in (SHARE, 2 * SHARE, 4 * SHARE):
                folded = folded + pltpu.roll(folded, step, 1)
            parts.append(folded)
        real, imag = parts
        fr, fi = filtr[half, 0], filtr[half, 1]
        filtered = jnp.concatenate([fr * real + fi * imag, fr * imag - fi * real], axis=1).astype(BF16)
        back = jnp.where(
            low_slots,
            jnp.dot(legt[0], filtered, preferred_element_type=F32),
            jnp.dot(legt[1], filtered, preferred_element_type=F32),
        )
        for part in range(2):
            wide = back[:, part * CH : (part + 1) * CH].reshape(LAT_DEV, ROWS, CH)
            wide = jnp.where(diagonal, wide, 0.0).astype(BF16)
            zed[half, :, pl.ds(part * CH, CH)] = wide.reshape(SLOTS, CH)
        returned = jnp.dot(pick[...], zed[half], preferred_element_type=F32)
        for q in range(2):
            coltmp[half, pl.ds(q, LAT_DEV, stride=2), :] = returned[:, q * CH : (q + 1) * CH]
        lat_s2[half] = coltmp[half].astype(BF16).reshape(LAT_DEV, 2, CH)
        all_lat(lat_s2.at[half], lat_r2.at[half], 2 + half)

    load_ti.wait()
    low_block = low_half(HALF)

    def block_of(p, half, modes):
        four = jnp.dot(tiv[p], modes, preferred_element_type=F32)
        first = four[:HALF] + pltpu.roll(four[HALF : 2 * HALF], CH - 8, 1)
        second = pltpu.roll(four[2 * HALF : 3 * HALF], 8, 1) + four[3 * HALF :]
        send2[half, p] = jnp.where(low_block, first, second).astype(BF16)

    own2 = []
    for half in range(2):
        pltpu.make_async_copy(lat_s2.at[half], lat_r2.at[half], lr.at[2 + half]).wait()
        modes = lat_r2[half].reshape(MODES, CH)
        for k in far_first:
            block_of(partner(k), half, modes)
            swap(send2, recv2, s2, r2, half, k).start()
        block_of(d, half, modes)
        own2.append(
            pltpu.make_async_copy(send2.at[half, d], recv2.at[half, d], own_sem.at[2 + half])
        )
        own2[half].start()

    load_kern.wait()
    kpad[...] = jnp.zeros_like(kpad)
    for t in range(TAPS):
        kpad[pl.ds(16 * t, KINDS), :] = kernv[t]
    above_slot = up * ROWS + rows_ref[up] - 1
    here = lax.broadcasted_iota(jnp.int32, (SLOTS, CH), 1)
    slot_row = lax.broadcasted_iota(jnp.int32, (SLOTS, CH), 0)
    source = jnp.where(here - 1 < live, a * ROWS + here - 1, down * ROWS)
    source = jnp.where(here == 0, above_slot, source)
    one_hot = jnp.where(slot_row == source, 1.0, 0.0)
    chosen = jnp.dot(kpad[...], one_hot, precision=lax.Precision.HIGHEST, preferred_element_type=F32)
    for row in range(ROWS + 2):
        kbc[row] = jnp.broadcast_to(chosen[:, row : row + 1], (16 * TAPS, CH))

    load_w.wait()
    wf[...] = wv[...].astype(F32)

    def weights(step, carry):
        row, half = step // 2, lax.rem(step, 2)
        o = pl.multiple_of(half * 64, 64)
        for t in range(TAPS):
            total = None
            for k in range(KINDS):
                part = wf[k, pl.ds(o, 64), :] * kbc[row, pl.ds(16 * t + k, 1), :]
                total = part if total is None else total + part
            tap_row, tap_col = t // 3, t % 3
            weff[row, pl.ds(tap_col * CH + o, 64), pl.ds(tap_row * CH, CH)] = total.astype(BF16)
        return carry

    lax.fori_loop(0, 2 * (ROWS + 2), weights, 0)

    for copy in edges:
        copy.wait()
    has_above = a > 0
    has_below = a < LAT_DEV - 1
    above_row = jnp.where(has_above, row_r[0].astype(F32), 0.0)
    below_row = jnp.where(has_below, row_r[1].astype(F32), 0.0)
    ext[0, pl.ds(EDGE, LONP), :] = above_row
    for slot in range(1, ROWS):
        old = ext[slot + 1, pl.ds(EDGE, LONP), :]
        ext[slot + 1, pl.ds(EDGE, LONP), :] = jnp.where(live == slot, below_row, old)
    ext[ROWS + 1, pl.ds(EDGE, LONP), :] = jnp.where(live == ROWS, below_row, 0.0)
    for side, at in ((0, EDGE - 1), (1, EDGE + LON)):
        slots = cell_r[side].astype(F32)
        above_cell = jnp.where(has_above, cell_r[2 + side].astype(F32), 0.0)
        below_cell = jnp.where(has_below, cell_r[4 + side].astype(F32), 0.0)
        ext[0, pl.ds(at, 1), :] = above_cell[0:1]
        for slot in range(ROWS + 1):
            edge_cell = jnp.where(live == slot, below_cell[0:1], slots[slot : slot + 1])
            ext[slot + 1, pl.ds(at, 1), :] = edge_cell

    for spare in (0, 1, ROWS + 2, ROWS + 3):
        dsum[spare] = jnp.zeros((LONP, CH), F32)

    def stencil(row, carry):
        field = jnp.concatenate(
            [ext[row, pl.ds(EDGE - b, LONP), :] for b in (-1, 0, 1)], axis=1
        ).astype(BF16)
        taps = jnp.dot(field, weff[row], preferred_element_type=F32)
        for step in (-1, 0, 1):
            index = (step + 1) * CH
            dsum[row + step + 1] += taps[:, index : index + CH]
        return carry

    lax.fori_loop(0, ROWS + 2, stencil, 0)

    for half in range(2):
        own2[half].wait()
        for k in far_first:
            swap(send2, recv2, s2, r2, half, k).wait()
    for chunk in range(HALF // 16):
        begin = chunk * 16
        blocks = ([], [])
        for e in range(LON_DEV):
            one = recv2[0, e, pl.ds(begin, 16), :].astype(F32)
            two = recv2[1, e, pl.ds(begin, 16), :].astype(F32)
            blocks[0].append(jnp.where(low16, one, pltpu.roll(two, 8, 1)))
            blocks[1].append(jnp.where(low16, pltpu.roll(one, CH - 8, 1), two))
        for half in range(2):
            first = half * HALF + begin
            rows = exchange_groups(blocks[half], group16)
            for r in range(ROWS):
                total = dsum[r + 2, pl.ds(first, 16), :]
                total = total + rows[r] * qw_ref[a * ROWS + r]
                total = jnp.where(r < live, total, 0.0)
                outf[pl.ds(first * ROWS + r, 16, stride=ROWS), :] = total
    out_ref[...] = outf[pl.ds(0, LON * ROWS), :].astype(BF16).reshape(LON, ROWS, CH)

    for half in range(2):
        for which, sent in ((half, lat_s1), (2 + half, lat_s2)):
            most = sent.at[half, pl.ds(0, LAT_DEV - 1)]
            pltpu.make_async_copy(most, most, ls.at[which]).wait()


def on_device(grad_output, band_rows, legendre, quad_weights, spectral_filter, disco_kernel, disco_weight):
    forward, inverse = trig_tables()
    any_space = pl.BlockSpec(memory_space=pl.ANY)
    vmem = pltpu.VMEM
    dma = pltpu.SemaphoreType.DMA
    out = pl.pallas_call(
        kernel,
        out_shape=jax.ShapeDtypeStruct((LON, ROWS, CH), BF16),
        in_specs=[pl.BlockSpec(memory_space=pltpu.SMEM)] * 2 + [any_space] * 7,
        out_specs=pl.BlockSpec(memory_space=pltpu.VMEM),
        scratch_shapes=[
            vmem((LON, ROWS, CH), BF16),
            vmem((LONP * ROWS, CH), F32),
            vmem((ROWS + 2, LONP + 2 * EDGE, CH), F32),
            vmem((2, LON_DEV, HALF, CH), BF16),
            vmem((2, LON_DEV, HALF, CH), BF16),
            vmem((2, LAT_DEV, 2, CH), BF16),
            vmem((2, LAT_DEV, 2, CH), BF16),
            vmem((2, LAT_DEV, 2, CH), BF16),
            vmem((2, LAT_DEV, 2, CH), BF16),
            vmem((2, LON_DEV, HALF, CH), BF16),
            vmem((2, LON_DEV, HALF, CH), BF16),
            vmem((2, LONP, CH), BF16),
            vmem((2, LONP, CH), BF16),
            vmem((6, 16, CH), BF16),
            vmem((6, 16, CH), BF16),
            vmem((2, DEG, SLOTS), F32),
            vmem((2, DEGP, SLOTS), BF16),
            vmem((2, SLOTS, DEGP), BF16),
            vmem((2, DEG, CH), F32),
            vmem((2, 2, DEGP, CH), F32),
            vmem((TAPS, KINDS, SLOTS), F32),
            vmem((16 * TAPS, SLOTS), F32),
            vmem((ROWS + 2, 16 * TAPS, CH), F32),
            vmem((KINDS, CH, CH), BF16),
            vmem((KINDS, CH, CH), F32),
            vmem((ROWS + 2, 3 * CH, 3 * CH), BF16),
            vmem((2, COEF, LON_DEV * HALF), BF16),
            vmem((LON_DEV, 4 * HALF, MODES), BF16),
            vmem((ROWS + 4, LONP, CH), F32),
            vmem((2, 2 * LAT_DEV, CH), F32),
            vmem((2, SLOTS, 2 * CH), BF16),
            vmem((2, SLOTS, 2 * CH), BF16),
            vmem((LAT_DEV, SLOTS), BF16),
            vmem((LONP * ROWS, CH), F32),
            dma((8,)),
            dma((4,)),
            dma((2, 8)),
            dma((2, 8)),
            dma((2, 8)),
            dma((2, 8)),
            dma((8,)),
            dma((8,)),
            dma((4,)),
            dma((4,)),
        ],
        compiler_params=pltpu.CompilerParams(
            collective_id=0, has_side_effects=True, vmem_limit_bytes=56 * 2**20
        ),
    )(
        band_rows,
        quad_weights,
        jnp.transpose(grad_output, (1, 0, 2)),
        legendre,
        spectral_filter,
        jnp.transpose(disco_kernel, (1, 2, 0)),
        jnp.transpose(disco_weight, (1, 0, 2)),
        jnp.asarray(forward),
        jnp.asarray(inverse),
    )
    return jnp.transpose(out, (1, 0, 2))


def solution(mesh):
    placed = (P("lat", "lon", None), P(), P("lat", None, None), P(), P(), P(), P())
    return jax.shard_map(
        on_device, mesh=mesh, in_specs=placed, out_specs=P("lat", "lon", None), check_vma=False
    )
```
